512 devices in a mesh: gz: 2 (over y_lo), gy: 8 (over y_hi, core), gx: 32 (over x, z).
Axes of the slice: x: 4, y: 8 (y_hi: 4, y_lo: 2; y = y_hi * 2 + y_lo), z: 8, core: 2. Of those that a mesh axis runs over, the one named last changes fastest.
Arguments:
- volume: float32 [128, 256, 256], P('gx', 'gy', 'gz'), may hold values from -6 to 6
- thresholds: float32 [3, 7], replicated, may hold values from 0.02 to 0.4
Outputs:
- denoised: float32 [128, 256, 256], P('gx', 'gy', 'gz')
The draws below stay inside these ranges and needn't reach their ends.
All inputs are finite; a program needn't handle non-finite values.
Results may differ from the reference program's by a relative error of at most 0.0003.
Values sent between devices are 32-bit elements; how exact they have to be, the bound alone decides.
A program may use at most 64 MiB of HBM per device.

```python
import math
import jax
import jax.numpy as jnp
from jax import lax

LEVELS = 3
NX = 128
NY = 256
NZ = 256


def levels(own_key, dims, pieces, least, top_value):
    def one(position, blocks):
        steps = jax.random.uniform(jax.random.fold_in(jax.random.fold_in(own_key, 6), position), (blocks,), jnp.float32, least / len(pieces), top_value / len(pieces))
        return jnp.repeat(jnp.exp(steps), dims[position] // blocks).reshape((-1,) + (1,) * (len(dims) - position - 1))

    gain = one(*pieces[0])
    for cut in pieces[1:]:
        gain = gain * one(*cut)
    return gain


def scatter_about(stream_key, shape, deviation, reach, cuts=(), held_as=jnp.bfloat16):
    entries = jax.random.normal(stream_key, shape, jnp.float32) * deviation
    if len(cuts) > 0:
        entries = levels(stream_key, shape, cuts, -0.22, 0.18) * entries
    return jnp.clip(entries, min=-reach, max=reach).astype(held_as)


def setup_inputs(seed: int = 0) -> dict:
    arg_keys = jax.random.split(jax.random.key(seed), 3)
    volume = scatter_about(arg_keys[0], (NX, NY, NZ), 1.0, 6.0, ((0, 32), (1, 8), (2, 2)), jnp.float32)
    thresholds = jnp.clip(jnp.exp(jax.random.uniform(arg_keys[1], (LEVELS, 7), jnp.float32, math.log(0.02), math.log(0.4))), 0.02, 0.4)
    return {"volume": volume, "thresholds": thresholds}


base_taps = [0.23037781330885523, 0.7148465705525415, 0.6308807679295904, -0.02798376941698385, -0.18703481171888114, 0.030841381835986965, 0.032883011666982945, -0.010597401784997278]
scaling_taps = [value / math.sqrt(2.0) for value in base_taps]
wavelet_taps = [(-1.0) ** index * base_taps[7 - index] / math.sqrt(2.0) for index in range(8)]

def padded_copy(field, dim, width):
    padding = [(0, 0)] * field.ndim
    padding[dim] = (width, width)
    return jnp.pad(field, padding)

def split_pair(field, dim, step):
    width = 4 * step
    ext = padded_copy(field, dim, width)
    count = field.shape[dim]
    smooth = jnp.zeros_like(field)
    detail = jnp.zeros_like(field)
    for index in range(8):
        offset = width + (index - 3) * step
        piece = lax.slice_in_dim(ext, offset, offset + count, axis=dim)
        smooth = smooth + scaling_taps[index] * piece
        detail = detail + wavelet_taps[index] * piece
    return (smooth, detail)

def merge_pair(smooth, detail, dim, step):
    width = 4 * step
    ext_low = padded_copy(smooth, dim, width)
    ext_high = padded_copy(detail, dim, width)
    count = smooth.shape[dim]
    total = jnp.zeros_like(smooth)
    for index in range(8):
        offset = width - (index - 3) * step
        total = total + scaling_taps[index] * lax.slice_in_dim(ext_low, offset, offset + count, axis=dim)
        total = total + wavelet_taps[index] * lax.slice_in_dim(ext_high, offset, offset + count, axis=dim)
    return total

def subbands(field, step):
    bands = []
    for part in split_pair(field, 0, step):
        for inner in split_pair(part, 1, step):
            for last in split_pair(inner, 2, step):
                bands.append(last)
    return bands

def reference(volume, thresholds):
    approx = [volume]
    for level in range(LEVELS):
        approx.append(subbands(approx[-1], 2 ** level)[0])
    recon = approx[LEVELS]
    for level in range(LEVELS - 1, -1, -1):
        step = 2 ** level
        bands = subbands(approx[level], step)
        coeffs = [recon]
        for band in range(1, 8):
            value = bands[band]
            coeffs.append(jnp.sign(value) * jnp.maximum(jnp.abs(value) - thresholds[level, band - 1], 0.0))
        quads = [merge_pair(coeffs[2 * i], coeffs[2 * i + 1], 2, step) for i in range(4)]
        pairs = [merge_pair(quads[2 * i], quads[2 * i + 1], 1, step) for i in range(2)]
        recon = merge_pair(pairs[0], pairs[1], 0, step)
    return recon
```

```python
import math

import jax
import jax.numpy as jnp
import ml_dtypes
import numpy as np
from jax import lax
from jax.experimental import pallas as pl
from jax.experimental.pallas import tpu as pltpu
from jax.sharding import PartitionSpec as P

MESH = pl.DeviceIdType.MESH
LEVELS = 3
NX, NY, NZ = 128, 256, 256
GX, GY, GZ = 32, 8, 2
CELLS = NX // GX
ROWS = NY // GY
HALF = NZ // GZ
OWN = ROWS // GZ

base_taps = [
    0.23037781330885523,
    0.7148465705525415,
    0.6308807679295904,
    -0.02798376941698385,
    -0.18703481171888114,
    0.030841381835986965,
    0.032883011666982945,
    -0.010597401784997278,
]
scaling_taps = [value / math.sqrt(2.0) for value in base_taps]
wavelet_taps = [(-1.0) ** index * base_taps[7 - index] / math.sqrt(2.0) for index in range(8)]

FAR_LOW, FAR_HIGH = -6, 7
REACH = ((-1, 1), (-3, 3), (FAR_LOW, FAR_HIGH))
LOW = (8, 16, 24)
SPAN = (32, 48, 72)
PADDED = (32, 48, 80)


def chains(count):
    def banded(taps, step):
        out = np.zeros((count, count))
        for index, tap in enumerate(taps):
            offset = (index - 3) * step
            rows = np.arange(max(0, -offset), min(count, count - offset))
            out[rows, rows + offset] = tap
        return out

    so_far, result = np.eye(count), []
    for level in range(LEVELS):
        low = banded(scaling_taps, 2**level) @ so_far
        high = banded(wavelet_taps, 2**level) @ so_far
        result.append((low, high))
        so_far = low
    return result


def two_parts(table):
    high = table.astype(ml_dtypes.bfloat16)
    low = (table - high.astype(np.float64)).astype(ml_dtypes.bfloat16)
    return high, low


def tables():
    columns = np.zeros((GX, (FAR_HIGH - FAR_LOW + 1) * CELLS, 128), np.float32)
    for level, pair in enumerate(chains(NX)):
        for band, matrix in enumerate(pair):
            for device in range(GX):
                for cell in range(CELLS):
                    for place in range(columns.shape[1]):
                        source = (device + FAR_LOW) * CELLS + place
                        if 0 <= source < NX:
                            columns[device, place, level * 8 + band * 4 + cell] = matrix[
                                device * CELLS + cell, source
                            ]
    down = np.zeros((GY * GZ, LEVELS, 2 * 2 * OWN, 128), ml_dtypes.bfloat16)
    up = np.zeros((GY * GZ, LEVELS, 2 * PADDED[2], 128), ml_dtypes.bfloat16)
    for level, pair in enumerate(chains(NY)):
        for device in range(GY * GZ):
            window = np.zeros((2, OWN, PADDED[level]))
            for place in range(SPAN[level]):
                source = device * OWN - LOW[level] + place
                if 0 <= source < NY:
                    for band in range(2):
                        window[band, :, place] = pair[band][
                            device * OWN : device * OWN + OWN, source
                        ]
            window = window.reshape(2 * OWN, PADDED[level])
            for part, value in enumerate(two_parts(window)):
                down[device, level, part * 2 * OWN : (part + 1) * 2 * OWN, : PADDED[level]] = value
                first = part * PADDED[level]
                up[device, level, first : first + PADDED[level], : 2 * OWN] = value.T
    depth = np.zeros((LEVELS, 2, NZ, 2 * NZ), ml_dtypes.bfloat16)
    depth_back = np.zeros((LEVELS, 2, 2 * NZ, NZ), ml_dtypes.bfloat16)
    for level, pair in enumerate(chains(NZ)):
        both = np.concatenate(pair, axis=0)
        for part, value in enumerate(two_parts(both)):
            depth_back[level, part] = value
            depth[level, part] = value.T
    return columns, down, up, depth, depth_back


def segments(level, half):
    start = half * OWN - LOW[level]
    stop = start + SPAN[level]
    pieces = []
    for block in (-1, 0, 1):
        low, high = max(start, block * ROWS), min(stop, (block + 1) * ROWS)
        if low < high:
            pieces.append((block, low - block * ROWS, high - low, low - start))
    return pieces


def split(value):
    high = value.astype(jnp.bfloat16)
    return high, (value - high.astype(jnp.float32)).astype(jnp.bfloat16)


def dot(a, b):
    return jnp.dot(a, b, preferred_element_type=jnp.float32)


PIECES = [(g, s) for g in range(GZ) for s in range(3)]


def kernel(
    limits,
    volume,
    columns_hbm,
    down_hbm,
    up_hbm,
    depth_hbm,
    back_hbm,
    result,
    columns,
    down,
    up,
    depth,
    back,
    blocks,
    stacks,
    window0,
    window1,
    window2,
    spread0,
    spread1,
    spread2,
    landed,
    rows_in,
    bands,
    shrunk_high,
    shrunk_low,
    rows_out,
    starts,
    sums,
    load_sem,
    block_send,
    block_recv,
    row_send,
    row_recv,
    back_send,
    back_recv,
    sum_send,
    sum_recv,
):
    gz, gy, gx = lax.axis_index("gz"), lax.axis_index("gy"), lax.axis_index("gx")
    windows = (window0, window1, window2)
    spreads = (spread0, spread1, spread2)

    def column_peer(distance):
        return (gz, gy, lax.rem(gx + distance + GX, GX))

    def row_peer(block, half):
        return (half, lax.rem(gy + block + GY, GY), gx)

    place = gy * GZ + gz
    loads = [
        pltpu.make_async_copy(source, target, load_sem.at[index])
        for index, (source, target) in enumerate(
            (
                (columns_hbm.at[gx], columns),
                (down_hbm.at[place], down),
                (up_hbm.at[place], up),
                (depth_hbm, depth),
                (back_hbm, back),
            )
        )
    ]
    for load in loads:
        load.start()

    barrier = pltpu.get_barrier_semaphore()
    peers = [column_peer(d) for d in (-7, -6, -1, 1, 6, 7)]
    peers += [row_peer(block, half) for block in (-1, 1) for half in range(GZ)]
    peers.append(row_peer(0, 1 - gz))
    for peer in peers:
        pl.semaphore_signal(barrier, inc=1, device_id=peer, device_id_type=MESH)
    pl.semaphore_wait(barrier, len(peers))

    def slot(d):
        return blocks.at[d - FAR_LOW]

    def pass_on(d, distance):
        target = d - distance
        copy = pltpu.make_async_remote_copy(
            src_ref=volume if d == 0 else slot(d),
            dst_ref=slot(target),
            send_sem=block_send.at[target - FAR_LOW],
            recv_sem=block_recv.at[target - FAR_LOW],
            device_id=column_peer(distance),
            device_id_type=MESH,
        )
        copy.start()
        copies[target] = copy

    copies = {}
    pass_on(0, 1)
    pass_on(0, -1)
    pass_on(0, -7)
    pass_on(0, 6)
    loads[0].wait()

    def add_block(d, fresh=False):
        source = volume if d == 0 else slot(d)
        for level in range(LEVELS):
            if not REACH[level][0] <= d <= REACH[level][1]:
                continue

            def one(index, carry, level=level):
                total = None
                for cell in range(CELLS):
                    weight = columns[(d - FAR_LOW) * CELLS + cell, level * 8 + index]
                    term = weight * source[cell]
                    total = term if total is None else total + term
                if not fresh:
                    total = total + stacks[level, index]
                stacks[level, index] = total
                return carry

            lax.fori_loop(0, 8, one, 0)

    def row_copy(level, half, piece, self_too):
        block, first, count, into = piece
        return dict(
            src_ref=stacks.at[level, :, pl.ds(first, count)],
            dst_ref=windows[level].at[gz, :, pl.ds(into, count)],
        ), row_recv.at[level, gz, block + 1]

    def send_rows(level):
        for half in range(GZ):
            for piece in segments(level, half):
                block, first, count, into = piece
                source = stacks.at[level, :, pl.ds(first, count)]
                target = windows[level].at[gz, :, pl.ds(into, count)]
                recv = row_recv.at[level, gz, block + 1]
                remote = pltpu.make_async_remote_copy(
                    src_ref=source,
                    dst_ref=target,
                    send_sem=row_send.at[level, half, block + 1],
                    recv_sem=recv,
                    device_id=row_peer(-block, half),
                    device_id_type=MESH,
                )
                if block != 0:
                    remote.start()
                else:
                    pl.when(gz != half)(remote.start)
                    pl.when(gz == half)(pltpu.make_async_copy(source, target, recv).start)

    def wait_rows(level):
        for half in range(GZ):

            @pl.when(gz == half)
            def _(half=half):
                for block, _, count, into in segments(level, half):
                    for source in range(GZ):
                        target = windows[level].at[source, :, pl.ds(into, count)]
                        recv = row_recv.at[level, source, block + 1]
                        pltpu.make_async_copy(target, target, recv).wait()

    def wait_rows_sent(level):
        for half in range(GZ):
            for block, first, count, into in segments(level, half):
                source = stacks.at[level, :, pl.ds(first, count)]
                sent = pltpu.make_async_copy(source, source, row_send.at[level, half, block + 1])
                if block != 0:
                    sent.wait()
                else:
                    pl.when(gz != half)(sent.wait)

    add_block(0, fresh=True)
    copies[-1].wait_recv()
    pass_on(-1, 1)
    copies[1].wait_recv()
    pass_on(1, -1)
    add_block(-1)
    add_block(1)
    send_rows(0)
    copies[7].wait_recv()
    pass_on(7, 1)
    copies[-6].wait_recv()
    pass_on(-6, -1)
    add_block(7)
    add_block(-6)
    copies[-2].wait_recv()
    pass_on(-2, 1)
    copies[2].wait_recv()
    pass_on(2, -1)
    add_block(-2)
    add_block(2)
    copies[6].wait_recv()
    pass_on(6, 1)
    copies[-5].wait_recv()
    add_block(6)
    add_block(-5)
    copies[-3].wait_recv()
    pass_on(-3, 1)
    copies[3].wait_recv()
    pass_on(3, -1)
    add_block(-3)
    add_block(3)
    send_rows(1)
    copies[5].wait_recv()
    add_block(5)
    copies[-4].wait_recv()
    add_block(-4)
    copies[4].wait_recv()
    add_block(4)
    send_rows(2)

    for load in loads[1:]:
        load.wait()

    def shrink_level(level):
        span, padded = SPAN[level], PADDED[level]

        def rows_forth(index, carry):
            data = jnp.concatenate([windows[level][0, index], windows[level][1, index]], axis=1)
            if padded > span:
                data = jnp.concatenate(
                    [data, jnp.zeros((padded - span, NZ), jnp.float32)], axis=0
                )
            high, low = split(data)
            weights = down[level][:, :padded]
            both = dot(weights, high)
            total = both[: 2 * OWN] + both[2 * OWN :] + dot(weights[: 2 * OWN], low)
            rows_in[pl.ds(pl.multiple_of(index * 2 * OWN, 2 * OWN), 2 * OWN)] = total
            return carry

        lax.fori_loop(0, 8, rows_forth, 0)
        high, low = split(rows_in[...])
        bands[...] = (
            dot(high, depth[level, 0]) + dot(low, depth[level, 0]) + dot(high, depth[level, 1])
        )

        def shrink(index, carry):
            stack = index // 4
            for row_band in range(2):
                first = pl.multiple_of(index * 2 * OWN + row_band * OWN, OWN)
                for depth_band in range(2):
                    number = 4 * stack + 2 * row_band + depth_band
                    limit = limits[level, jnp.maximum(number - 1, 0)]
                    if row_band == 0 and depth_band == 0:
                        none = 0.0 if level == LEVELS - 1 else jnp.inf
                        limit = jnp.where(stack == 0, jnp.float32(none), limit)
                    spot = (pl.ds(first, OWN), pl.ds(depth_band * NZ, NZ))
                    value = bands[spot]
                    value = value - jnp.clip(value, -limit, limit)
                    shrunk_high[spot], shrunk_low[spot] = split(value)
            return carry

        lax.fori_loop(0, 8, shrink, 0)
        rows_out[...] = (
            dot(shrunk_high[...], back[level, 0])
            + dot(shrunk_low[...], back[level, 0])
            + dot(shrunk_high[...], back[level, 1])
        )

        def rows_back(index, carry):
            high, low = split(rows_out[pl.ds(pl.multiple_of(index * 2 * OWN, 2 * OWN), 2 * OWN)])
            weights = up[level][: 2 * padded, : 2 * OWN]
            both = dot(weights, high)
            total = both[:padded] + both[padded:] + dot(weights[:padded], low)
            spreads[level][0, index] = total[:span, :HALF]
            spreads[level][1, index] = total[:span, HALF:]
            return carry

        lax.fori_loop(0, 8, rows_back, 0)

    def back_copies(level, half):
        for block, first, count, into in segments(level, half):
            for depth_half in range(GZ):
                source = spreads[level].at[depth_half, :, pl.ds(into, count)]
                target = landed.at[level, half, block + 1, :, pl.ds(0, count)]
                recv = back_recv.at[level, half, block + 1]
                if block == 0 and depth_half == half:
                    yield pltpu.make_async_copy(source, target, recv), False
                else:
                    yield pltpu.make_async_remote_copy(
                        src_ref=source,
                        dst_ref=target,
                        send_sem=back_send.at[level, depth_half, block + 1],
                        recv_sem=recv,
                        device_id=row_peer(block, depth_half),
                        device_id_type=MESH,
                    ), True

    def send_back(level):
        for half in range(GZ):

            @pl.when(gz == half)
            def _(half=half):
                for copy, _ in back_copies(level, half):
                    copy.start()

    def wait_back_sent(level):
        for half in range(GZ):

            @pl.when(gz == half)
            def _(half=half):
                for copy, remote in back_copies(level, half):
                    if remote:
                        copy.wait_send()

    def gather_back(level):
        pieces = [(half, piece) for half in range(GZ) for piece in segments(level, half)]
        for half, (block, _, count, _) in pieces:
            target = landed.at[level, half, block + 1, :, pl.ds(0, count)]
            pltpu.make_async_copy(target, target, back_recv.at[level, half, block + 1]).wait()

        def one(index, carry):
            groups = []
            for group in range(ROWS // 8):
                total = None
                for half, (block, first, count, _) in pieces:
                    if first <= group * 8 < first + count:
                        term = landed[level, half, block + 1, index, pl.ds(group * 8 - first, 8)]
                        total = term if total is None else total + term
                groups.append(total)
            for group, total in enumerate(groups):
                stacks[level, index, pl.ds(group * 8, 8)] = total
            return carry

        lax.fori_loop(0, 8, one, 0)

    wait_rows(0)
    shrink_level(0)
    wait_rows(1)
    shrink_level(1)
    wait_rows(2)
    shrink_level(2)
    send_back(2)
    send_back(1)
    send_back(0)
    for level in range(LEVELS):
        wait_rows_sent(level)
    gather_back(2)

    def fill(target, d, arrived=None):
        def one(cell, carry):
            total = None if arrived is None else arrived[cell]
            for level in range(LEVELS):
                if not REACH[level][0] <= d <= REACH[level][1]:
                    continue
                for index in range(8):
                    weight = columns[(d - FAR_LOW) * CELLS + cell, level * 8 + index]
                    term = weight * stacks[level, index]
                    total = term if total is None else total + term
            target[cell] = total
            return carry

        lax.fori_loop(0, CELLS, one, 0)

    UP3, UP2, UP1, UP0, DN3, DN2, DN1, DN0, HI6, HI7, HI0, LO6, LO0 = range(13)
    moved = []

    def hand_on(source, target, distance):
        copy = pltpu.make_async_remote_copy(
            src_ref=source,
            dst_ref=sums.at[target],
            send_sem=sum_send.at[target],
            recv_sem=sum_recv.at[target],
            device_id=column_peer(distance),
            device_id_type=MESH,
        )
        copy.start()
        moved.append(copy)

    def arrived(target):
        spot = sums.at[target]
        pltpu.make_async_copy(spot, spot, sum_recv.at[target]).wait()
        return spot

    def add_and_hand_on(which, d, target, distance):
        spot = arrived(which)
        fill(spot, d, spot)
        hand_on(spot, target, distance)

    fill(starts.at[0], 4)
    hand_on(starts.at[0], UP3, 1)
    fill(starts.at[1], -4)
    hand_on(starts.at[1], DN3, -1)
    fill(starts.at[2], 5)
    hand_on(starts.at[2], HI6, -1)
    fill(starts.at[3], -5)
    hand_on(starts.at[3], LO6, 1)
    gather_back(1)
    add_and_hand_on(UP3, 3, UP2, 1)
    add_and_hand_on(DN3, -3, DN2, -1)
    add_and_hand_on(HI6, 6, HI7, -1)
    add_and_hand_on(LO6, -6, LO0, -6)
    gather_back(0)
    add_and_hand_on(UP2, 2, UP1, 1)
    add_and_hand_on(DN2, -2, DN1, -1)
    add_and_hand_on(HI7, 7, HI0, 7)
    fill(result, 0)
    add_and_hand_on(UP1, 1, UP0, 1)
    add_and_hand_on(DN1, -1, DN0, -1)
    last = [arrived(which) for which in (LO0, HI0, UP0, DN0)]
    result[...] = result[...] + last[0][...] + last[1][...] + last[2][...] + last[3][...]

    for copy in copies.values():
        copy.wait_send()
    for level in range(LEVELS):
        wait_back_sent(level)
    for copy in moved:
        copy.wait_send()


def per_device(volume, thresholds):
    columns, down, up, depth, back = tables()
    block = (CELLS, ROWS, HALF)
    f32, bf16 = jnp.float32, jnp.bfloat16
    vmem, dma = pltpu.VMEM, pltpu.SemaphoreType.DMA
    window_shapes = [vmem((GZ, 8, span, HALF), f32) for span in SPAN]
    count = FAR_HIGH - FAR_LOW + 1
    return pl.pallas_call(
        kernel,
        out_shape=jax.ShapeDtypeStruct(volume.shape, volume.dtype),
        in_specs=[
            pl.BlockSpec(memory_space=pltpu.SMEM),
            pl.BlockSpec(memory_space=pltpu.VMEM),
        ]
        + [pl.BlockSpec(memory_space=pl.ANY)] * 5,
        out_specs=pl.BlockSpec(memory_space=pltpu.VMEM),
        scratch_shapes=[
            pltpu.SMEM(columns.shape[1:], f32),
            vmem(down.shape[1:], bf16),
            vmem(up.shape[1:], bf16),
            vmem(depth.shape, bf16),
            vmem(back.shape, bf16),
            vmem((count,) + block, f32),
            vmem((LEVELS, 8, ROWS, HALF), f32),
            *window_shapes,
            *window_shapes,
            vmem((LEVELS, GZ, 3, 8, ROWS, HALF), f32),
            vmem((16 * OWN, NZ), f32),
            vmem((16 * OWN, 2 * NZ), f32),
            vmem((16 * OWN, 2 * NZ), bf16),
            vmem((16 * OWN, 2 * NZ), bf16),
            vmem((16 * OWN, NZ), f32),
            vmem((4,) + block, f32),
            vmem((13,) + block, f32),
            dma((5,)),
            dma((count,)),
            dma((count,)),
            dma((LEVELS, GZ, 3)),
            dma((LEVELS, GZ, 3)),
            dma((LEVELS, GZ, 3)),
            dma((LEVELS, GZ, 3)),
            dma((13,)),
            dma((13,)),
        ],
        compiler_params=pltpu.CompilerParams(
            collective_id=0, has_side_effects=True, vmem_limit_bytes=40 * 2**20
        ),
        name="shrinkage",
    )(thresholds, volume, columns, down, up, depth, back)


def solution(mesh):
    placed = (P("gx", "gy", "gz"), P())
    return jax.shard_map(
        per_device, mesh=mesh, in_specs=placed, out_specs=P("gx", "gy", "gz"), check_vma=False
    )
```

```python
import math

import jax
import jax.numpy as jnp
import ml_dtypes
import numpy as np
from jax import lax
from jax.experimental import pallas as pl
from jax.experimental.pallas import tpu as pltpu
from jax.sharding import PartitionSpec as P

MESH = pl.DeviceIdType.MESH
LEVELS = 3
NX, NY, NZ = 128, 256, 256
GX, GY, GZ = 32, 8, 2
CELLS = NX // GX
ROWS = NY // GY
HALF = NZ // GZ
OWN = ROWS // GZ

base_taps = [
    0.23037781330885523,
    0.7148465705525415,
    0.6308807679295904,
    -0.02798376941698385,
    -0.18703481171888114,
    0.030841381835986965,
    0.032883011666982945,
    -0.010597401784997278,
]
scaling_taps = [value / math.sqrt(2.0) for value in base_taps]
wavelet_taps = [(-1.0) ** index * base_taps[7 - index] / math.sqrt(2.0) for index in range(8)]

FAR_LOW, FAR_HIGH = -6, 7
REACH = ((-1, 1), (-3, 3), (FAR_LOW, FAR_HIGH))
LOW = (8, 16, 24)
SPAN = (32, 48, 72)
PADDED = (32, 48, 80)


def chains(count):
    def banded(taps, step):
        out = np.zeros((count, count))
        for index, tap in enumerate(taps):
            offset = (index - 3) * step
            rows = np.arange(max(0, -offset), min(count, count - offset))
            out[rows, rows + offset] = tap
        return out

    so_far, result = np.eye(count), []
    for level in range(LEVELS):
        low = banded(scaling_taps, 2**level) @ so_far
        high = banded(wavelet_taps, 2**level) @ so_far
        result.append((low, high))
        so_far = low
    return result


def two_parts(table):
    high = table.astype(ml_dtypes.bfloat16)
    low = (table - high.astype(np.float64)).astype(ml_dtypes.bfloat16)
    return high, low


def tables():
    columns = np.zeros((GX, (FAR_HIGH - FAR_LOW + 1) * CELLS, 128), np.float32)
    for level, pair in enumerate(chains(NX)):
        for band, matrix in enumerate(pair):
            for device in range(GX):
                for cell in range(CELLS):
                    for place in range(columns.shape[1]):
                        source = (device + FAR_LOW) * CELLS + place
                        if 0 <= source < NX:
                            columns[device, place, level * 8 + band * 4 + cell] = matrix[
                                device * CELLS + cell, source
                            ]
    down = np.zeros((GY * GZ, LEVELS, 2 * 2 * OWN, 128), ml_dtypes.bfloat16)
    up = np.zeros((GY * GZ, LEVELS, 2 * PADDED[2], 128), ml_dtypes.bfloat16)
    for level, pair in enumerate(chains(NY)):
        for device in range(GY * GZ):
            window = np.zeros((2, OWN, PADDED[level]))
            for place in range(SPAN[level]):
                source = device * OWN - LOW[level] + place
                if 0 <= source < NY:
                    for band in range(2):
                        window[band, :, place] = pair[band][
                            device * OWN : device * OWN + OWN, source
                        ]
            window = window.reshape(2 * OWN, PADDED[level])
            for part, value in enumerate(two_parts(window)):
                down[device, level, part * 2 * OWN : (part + 1) * 2 * OWN, : PADDED[level]] = value
                first = part * PADDED[level]
                up[device, level, first : first + PADDED[level], : 2 * OWN] = value.T
    depth = np.zeros((LEVELS, 2, NZ, 2 * NZ), ml_dtypes.bfloat16)
    depth_back = np.zeros((LEVELS, 2, 2 * NZ, NZ), ml_dtypes.bfloat16)
    for level, pair in enumerate(chains(NZ)):
        both = np.concatenate(pair, axis=0)
        for part, value in enumerate(two_parts(both)):
            depth_back[level, part] = value
            depth[level, part] = value.T
    return columns, down, up, depth, depth_back


def segments(level):
    start, stop = -LOW[level], SPAN[level] - LOW[level]
    pieces = []
    for block in (-2, -1, 1, 2):
        low, high = max(start, block * OWN), min(stop, (block + 1) * OWN)
        if low < high:
            pieces.append((block, low - block * OWN, high - low, low - start))
    return pieces


def split(value):
    high = value.astype(jnp.bfloat16)
    return high, (value - high.astype(jnp.float32)).astype(jnp.bfloat16)


def dot(a, b):
    return jnp.dot(a, b, preferred_element_type=jnp.float32)


def kernel(
    limits_hbm,
    volume_hbm,
    columns_hbm,
    down_hbm,
    up_hbm,
    depth_hbm,
    back_hbm,
    result,
    volume,
    limits,
    columns,
    down,
    up,
    depth,
    back,
    blocks,
    window0,
    window1,
    window2,
    spread0,
    spread1,
    spread2,
    landed,
    stacks,
    rows_in,
    bands,
    shrunk_high,
    shrunk_low,
    rows_out,
    starts,
    sums,
    finals,
    load_sem,
    first_send,
    first_recv,
    block_send,
    block_recv,
    row_send,
    row_recv,
    back_send,
    back_recv,
    sum_send,
    sum_recv,
    final_send,
    final_recv,
):
    gz, gy, gx = lax.axis_index("gz"), lax.axis_index("gy"), lax.axis_index("gx")
    pair, core = gy // 2, lax.rem(gy, 2)
    windows = (window0, window1, window2)
    spreads = (spread0, spread1, spread2)

    place = 4 * pair + 2 * gz + core
    at_home = gz == core

    def column_of(distance):
        return lax.rem(gx + distance + GX, GX)

    def column_peer(distance):
        return (gz, gy, column_of(distance))

    def worker(part, distance):
        return (core, 2 * pair + part, column_of(distance))

    def holder(half, distance):
        return (half, 2 * pair + gz, column_of(distance))

    def row_peer(block):
        other = lax.rem(place + block + 16, 16)
        return (lax.rem(other // 2, 2), 2 * (other // 4) + lax.rem(other, 2), gx)

    loads = [
        pltpu.make_async_copy(source, target, load_sem.at[index])
        for index, (source, target) in enumerate(
            (
                (volume_hbm, volume),
                (columns_hbm.at[gx], columns),
                (limits_hbm, limits),
                (down_hbm.at[place], down),
                (up_hbm.at[place], up),
                (depth_hbm, depth),
                (back_hbm, back),
            )
        )
    ]
    for load in loads:
        load.start()

    barrier = pltpu.get_barrier_semaphore()

    def greet(peer):
        pl.semaphore_signal(barrier, inc=1, device_id=peer, device_id_type=MESH)

    for part in range(2):
        for distance in (-7, 6, -1, 1):
            greet(worker(part, distance))
            greet(holder(part, -distance))
        pl.when(jnp.logical_not(jnp.logical_and(at_home, core == part)))(
            lambda part=part: greet(worker(part, 0))
        )
        pl.when(jnp.logical_not(jnp.logical_and(at_home, gz == part)))(
            lambda part=part: greet(holder(part, 0))
        )
    for distance in (-1, 1):
        greet(column_peer(distance))
    for block in (-2, -1, 1, 2):
        greet(row_peer(block))
    pl.semaphore_wait(barrier, 26 - 2 * at_home.astype(jnp.int32))

    FIRST = {1: -1, -1: 1, -7: 7, 6: -6, 0: 0}
    ORDER = (0, -1, 1, 7, -6)

    def slot(d):
        return blocks.at[d - FAR_LOW]

    def depth_half(ref, half):
        if isinstance(half, int):
            return ref.at[:, :, half * HALF : (half + 1) * HALF]
        return ref.at[:, :, pl.ds(pl.multiple_of(half * HALF, HALF), HALF)]

    def first_copies(distance, part):
        target = FIRST[distance]
        source = volume.at[:, part * OWN : (part + 1) * OWN]
        into = depth_half(slot(target), gz)
        index = ORDER.index(target)
        remote = pltpu.make_async_remote_copy(
            src_ref=source,
            dst_ref=into,
            send_sem=first_send.at[index, part],
            recv_sem=first_recv.at[index, gz],
            device_id=worker(part, distance),
            device_id_type=MESH,
        )
        return remote, source, into, first_recv.at[index, gz]

    def start_first(distance):
        for part in range(2):
            remote, source, into, recv = first_copies(distance, part)
            if distance == 0:
                here = jnp.logical_and(at_home, core == part)
                pl.when(jnp.logical_not(here))(remote.start)

                @pl.when(here)
                def _(source=source, into=into, recv=recv):
                    pltpu.make_async_copy(source, into, recv).start()

            else:
                remote.start()

    def wait_first(target):
        for half in range(2):
            into = depth_half(slot(target), half)
            pltpu.make_async_copy(into, into, first_recv.at[ORDER.index(target), half]).wait()

    def wait_first_sent(distance):
        index = ORDER.index(FIRST[distance])
        for part in range(2):
            source = volume.at[:, part * OWN : (part + 1) * OWN]

            def wait(source=source, part=part):
                pltpu.make_async_copy(source, source, first_send.at[index, part]).wait()

            if distance == 0:
                pl.when(jnp.logical_not(jnp.logical_and(at_home, core == part)))(wait)
            else:
                wait()

    copies = {}

    def pass_on(d, distance):
        target = d - distance
        copy = pltpu.make_async_remote_copy(
            src_ref=slot(d),
            dst_ref=slot(target),
            send_sem=block_send.at[target - FAR_LOW],
            recv_sem=block_recv.at[target - FAR_LOW],
            device_id=column_peer(distance),
            device_id_type=MESH,
        )
        copy.start()
        copies[target] = copy

    def own_rows(level):
        return pl.ds(LOW[level], OWN)

    def add_block(d, fresh=False):
        source = slot(d)
        for level in range(LEVELS):
            if not REACH[level][0] <= d <= REACH[level][1]:
                continue

            def one(index, carry, level=level):
                total = None
                for cell in range(CELLS):
                    weight = columns[(d - FAR_LOW) * CELLS + cell, level * 8 + index]
                    term = weight * source[cell]
                    total = term if total is None else total + term
                if not fresh:
                    total = total + windows[level][index, own_rows(level)]
                windows[level][index, own_rows(level)] = total
                return carry

            lax.fori_loop(0, 8, one, 0)

    def row_copy(level, number, piece):
        block, first, count, into = piece
        return pltpu.make_async_remote_copy(
            src_ref=windows[level].at[:, pl.ds(LOW[level] + first, count)],
            dst_ref=windows[level].at[:, pl.ds(into, count)],
            send_sem=row_send.at[level, number],
            recv_sem=row_recv.at[level, number],
            device_id=row_peer(-block),
            device_id_type=MESH,
        )

    rows_sent = []

    def send_rows(level):
        for number, piece in enumerate(segments(level)):
            copy = row_copy(level, number, piece)
            copy.start()
            rows_sent.append((level, copy))

    def wait_rows(level):
        for owner, copy in rows_sent:
            if owner == level:
                copy.wait_recv()

    loads[0].wait()
    start_first(1)
    start_first(-1)
    start_first(0)
    start_first(-7)
    start_first(6)
    loads[1].wait()
    wait_first(-1)
    pass_on(-1, 1)
    wait_first(1)
    pass_on(1, -1)
    wait_first(0)
    add_block(0, fresh=True)
    add_block(-1)
    add_block(1)
    send_rows(0)
    wait_first(7)
    pass_on(7, 1)
    wait_first(-6)
    pass_on(-6, -1)
    add_block(7)
    add_block(-6)
    copies[-2].wait_recv()
    pass_on(-2, 1)
    copies[2].wait_recv()
    pass_on(2, -1)
    add_block(-2)
    add_block(2)
    copies[6].wait_recv()
    pass_on(6, 1)
    copies[-5].wait_recv()
    add_block(6)
    add_block(-5)
    copies[-3].wait_recv()
    pass_on(-3, 1)
    copies[3].wait_recv()
    pass_on(3, -1)
    add_block(-3)
    add_block(3)
    send_rows(1)
    copies[5].wait_recv()
    add_block(5)
    copies[-4].wait_recv()
    add_block(-4)
    copies[4].wait_recv()
    add_block(4)
    send_rows(2)

    for load in loads[2:]:
        load.wait()

    def shrink_level(level):
        span, padded = SPAN[level], PADDED[level]

        def rows_forth(index, carry):
            data = windows[level][index]
            if padded > span:
                data = jnp.concatenate(
                    [data, jnp.zeros((padded - span, NZ), jnp.float32)], axis=0
                )
            high, low = split(data)
            weights = down[level][:, :padded]
            both = dot(weights, high)
            total = both[: 2 * OWN] + both[2 * OWN :] + dot(weights[: 2 * OWN], low)
            rows_in[pl.ds(pl.multiple_of(index * 2 * OWN, 2 * OWN), 2 * OWN)] = total
            return carry

        lax.fori_loop(0, 8, rows_forth, 0)
        high, low = split(rows_in[...])
        bands[...] = (
            dot(high, depth[level, 0]) + dot(low, depth[level, 0]) + dot(high, depth[level, 1])
        )

        def shrink(index, carry):
            stack = index // 4
            for row_band in range(2):
                first = pl.multiple_of(index * 2 * OWN + row_band * OWN, OWN)
                for depth_band in range(2):
                    number = 4 * stack + 2 * row_band + depth_band
                    limit = limits[level, jnp.maximum(number - 1, 0)]
                    if row_band == 0 and depth_band == 0:
                        none = 0.0 if level == LEVELS - 1 else jnp.inf
                        limit = jnp.where(stack == 0, jnp.float32(none), limit)
                    spot = (pl.ds(first, OWN), pl.ds(depth_band * NZ, NZ))
                    value = bands[spot]
                    value = value - jnp.clip(value, -limit, limit)
                    shrunk_high[spot], shrunk_low[spot] = split(value)
            return carry

        lax.fori_loop(0, 8, shrink, 0)
        rows_out[...] = (
            dot(shrunk_high[...], back[level, 0])
            + dot(shrunk_low[...], back[level, 0])
            + dot(shrunk_high[...], back[level, 1])
        )

        def rows_back(index, carry):
            high, low = split(rows_out[pl.ds(pl.multiple_of(index * 2 * OWN, 2 * OWN), 2 * OWN)])
            weights = up[level][: 2 * padded, : 2 * OWN]
            both = dot(weights, high)
            total = both[:padded] + both[padded:] + dot(weights[:padded], low)
            spreads[level][index] = total[:span]
            return carry

        lax.fori_loop(0, 8, rows_back, 0)

    back_sent = []

    def send_back(level):
        for number, (block, _, count, into) in enumerate(segments(level)):
            copy = pltpu.make_async_remote_copy(
                src_ref=spreads[level].at[:, pl.ds(into, count)],
                dst_ref=landed.at[level, number, :, pl.ds(0, count)],
                send_sem=back_send.at[level, number],
                recv_sem=back_recv.at[level, number],
                device_id=row_peer(block),
                device_id_type=MESH,
            )
            copy.start()
            back_sent.append((level, copy))

    def gather_back(level):
        for owner, copy in back_sent:
            if owner == level:
                copy.wait_recv()

        def one(index, carry):
            for group in range(OWN // 8):
                total = spreads[level][index, pl.ds(LOW[level] + group * 8, 8)]
                for number, (_, first, count, _) in enumerate(segments(level)):
                    if first <= group * 8 < first + count:
                        total = total + landed[level, number, index, pl.ds(group * 8 - first, 8)]
                stacks[level, index, pl.ds(group * 8, 8)] = total
            return carry

        lax.fori_loop(0, 8, one, 0)

    wait_rows(0)
    shrink_level(0)
    send_back(0)
    wait_rows(1)
    shrink_level(1)
    send_back(1)
    wait_rows(2)
    shrink_level(2)
    send_back(2)
    gather_back(2)

    def fill(target, d, arrived=None):
        def one(cell, carry):
            total = None if arrived is None else arrived[cell]
            for level in range(LEVELS):
                if not REACH[level][0] <= d <= REACH[level][1]:
                    continue
                for index in range(8):
                    weight = columns[(d - FAR_LOW) * CELLS + cell, level * 8 + index]
                    term = weight * stacks[level, index]
                    total = term if total is None else total + term
            target[cell] = total
            return carry

        lax.fori_loop(0, CELLS, one, 0)

    UP3, UP2, UP1, DN3, DN2, DN1, HI6, HI7, LO6 = range(9)
    SAME, UP0, DN0, HI0, LO0 = range(5)
    moved = []

    def hand_on(source, target, distance):
        copy = pltpu.make_async_remote_copy(
            src_ref=source,
            dst_ref=sums.at[target],
            send_sem=sum_send.at[target],
            recv_sem=sum_recv.at[target],
            device_id=column_peer(distance),
            device_id_type=MESH,
        )
        copy.start()
        moved.append(copy)

    def arrived(target):
        spot = sums.at[target]
        pltpu.make_async_copy(spot, spot, sum_recv.at[target]).wait()
        return spot

    def add_and_hand_on(which, d, target, distance):
        spot = arrived(which)
        fill(spot, d, spot)
        hand_on(spot, target, distance)

    def deliver(source, which, distance):
        into = finals.at[which, :, pl.ds(pl.multiple_of(core * OWN, OWN), OWN)]
        for half in range(2):
            part = depth_half(source, half)
            remote = pltpu.make_async_remote_copy(
                src_ref=part,
                dst_ref=into,
                send_sem=final_send.at[which, half],
                recv_sem=final_recv.at[which, core],
                device_id=holder(half, distance),
                device_id_type=MESH,
            )
            if which == SAME:
                here = jnp.logical_and(at_home, gz == half)
                pl.when(jnp.logical_not(here))(remote.start)

                @pl.when(here)
                def _(part=part):
                    pltpu.make_async_copy(part, into, final_recv.at[which, core]).start()

            else:
                remote.start()

    def wait_delivered(which):
        for half in range(2):
            part = depth_half(starts.at[0], half)

            def wait(part=part, half=half):
                pltpu.make_async_copy(part, part, final_send.at[which, half]).wait()

            if which == SAME:
                pl.when(jnp.logical_not(jnp.logical_and(at_home, gz == half)))(wait)
            else:
                wait()

    def add_and_deliver(which, d, final, distance):
        spot = arrived(which)
        fill(spot, d, spot)
        deliver(spot, final, distance)

    fill(starts.at[0], 4)
    hand_on(starts.at[0], UP3, 1)
    fill(starts.at[1], -4)
    hand_on(starts.at[1], DN3, -1)
    fill(starts.at[2], 5)
    hand_on(starts.at[2], HI6, -1)
    fill(starts.at[3], -5)
    hand_on(starts.at[3], LO6, 1)
    gather_back(1)
    add_and_hand_on(UP3, 3, UP2, 1)
    add_and_hand_on(DN3, -3, DN2, -1)
    add_and_hand_on(HI6, 6, HI7, -1)
    add_and_deliver(LO6, -6, LO0, -6)
    gather_back(0)
    fill(starts.at[4], 0)
    deliver(starts.at[4], SAME, 0)
    add_and_hand_on(UP2, 2, UP1, 1)
    add_and_hand_on(DN2, -2, DN1, -1)
    add_and_deliver(HI7, 7, HI0, 7)
    add_and_deliver(UP1, 1, UP0, 1)
    add_and_deliver(DN1, -1, DN0, -1)
    total = None
    for which in (SAME, LO0, HI0, UP0, DN0):
        for part in range(2):
            spot = finals.at[which, :, pl.ds(part * OWN, OWN)]
            pltpu.make_async_copy(spot, spot, final_recv.at[which, part]).wait()
        total = finals[which] if total is None else total + finals[which]
    result[...] = total

    for distance in FIRST:
        wait_first_sent(distance)
    for copy in copies.values():
        copy.wait_send()
    for _, copy in rows_sent + back_sent:
        copy.wait_send()
    for copy in moved:
        copy.wait_send()
    for which in range(5):
        wait_delivered(which)


def per_device(volume, thresholds):
    columns, down, up, depth, back = tables()
    block = (CELLS, OWN, NZ)
    f32, bf16 = jnp.float32, jnp.bfloat16
    vmem, dma = pltpu.VMEM, pltpu.SemaphoreType.DMA
    window_shapes = [vmem((8, span, NZ), f32) for span in SPAN]
    count = FAR_HIGH - FAR_LOW + 1
    return pl.pallas_call(
        kernel,
        out_shape=pltpu.VMEM(volume.shape, volume.dtype),
        in_specs=[pl.BlockSpec(memory_space=pltpu.HBM)] * 7,
        out_specs=pl.BlockSpec(memory_space=pltpu.VMEM),
        scratch_shapes=[
            vmem(volume.shape, f32),
            pltpu.SMEM(thresholds.shape, f32),
            pltpu.SMEM(columns.shape[1:], f32),
            vmem(down.shape[1:], bf16),
            vmem(up.shape[1:], bf16),
            vmem(depth.shape, bf16),
            vmem(back.shape, bf16),
            vmem((count,) + block, f32),
            *window_shapes,
            *window_shapes,
            vmem((LEVELS, 4, 8, OWN, NZ), f32),
            vmem((LEVELS, 8, OWN, NZ), f32),
            vmem((16 * OWN, NZ), f32),
            vmem((16 * OWN, 2 * NZ), f32),
            vmem((16 * OWN, 2 * NZ), bf16),
            vmem((16 * OWN, 2 * NZ), bf16),
            vmem((16 * OWN, NZ), f32),
            vmem((5,) + block, f32),
            vmem((9,) + block, f32),
            vmem((5,) + volume.shape, f32),
            dma((7,)),
            dma((5, 2)),
            dma((5, 2)),
            dma((count,)),
            dma((count,)),
            dma((LEVELS, 4)),
            dma((LEVELS, 4)),
            dma((LEVELS, 4)),
            dma((LEVELS, 4)),
            dma((9,)),
            dma((9,)),
            dma((5, 2)),
            dma((5, 2)),
        ],
        compiler_params=pltpu.CompilerParams(
            collective_id=0, has_side_effects=True, vmem_limit_bytes=60 * 2**20
        ),
        name="shrinkage",
    )(thresholds, volume, columns, down, up, depth, back)


def solution(mesh):
    placed = (P("gx", "gy", "gz"), P())
    return jax.shard_map(
        per_device, mesh=mesh, in_specs=placed, out_specs=P("gx", "gy", "gz"), check_vma=False
    )
```

```python
import math

import jax
import jax.numpy as jnp
import ml_dtypes
import numpy as np
from jax import lax
from jax.experimental import pallas as pl
from jax.experimental.pallas import tpu as pltpu
from jax.sharding import PartitionSpec as P

MESH = pl.DeviceIdType.MESH
LEVELS = 3
NX, NY, NZ = 128, 256, 256
GX, GY, GZ = 32, 8, 2
CELLS = NX // GX
ROWS = NY // GY
HALF = NZ // GZ
OWN = ROWS // GZ

base_taps = [
    0.23037781330885523,
    0.7148465705525415,
    0.6308807679295904,
    -0.02798376941698385,
    -0.18703481171888114,
    0.030841381835986965,
    0.032883011666982945,
    -0.010597401784997278,
]
scaling_taps = [value / math.sqrt(2.0) for value in base_taps]
wavelet_taps = [(-1.0) ** index * base_taps[7 - index] / math.sqrt(2.0) for index in range(8)]

FAR_LOW, FAR_HIGH = -6, 7
REACH = ((-1, 1), (-3, 3), (FAR_LOW, FAR_HIGH))
LOW = (8, 16, 24)
SPAN = (32, 48, 72)
PADDED = (32, 48, 80)


def chains(count):
    def banded(taps, step):
        out = np.zeros((count, count))
        for index, tap in enumerate(taps):
            offset = (index - 3) * step
            rows = np.arange(max(0, -offset), min(count, count - offset))
            out[rows, rows + offset] = tap
        return out

    so_far, result = np.eye(count), []
    for level in range(LEVELS):
        low = banded(scaling_taps, 2**level) @ so_far
        high = banded(wavelet_taps, 2**level) @ so_far
        result.append((low, high))
        so_far = low
    return result


def two_parts(table):
    high = table.astype(ml_dtypes.bfloat16)
    low = (table - high.astype(np.float64)).astype(ml_dtypes.bfloat16)
    return high, low


def tables():
    columns = np.zeros((GX, (FAR_HIGH - FAR_LOW + 1) * CELLS, 128), np.float32)
    for level, pair in enumerate(chains(NX)):
        for band, matrix in enumerate(pair):
            for device in range(GX):
                for cell in range(CELLS):
                    for place in range(columns.shape[1]):
                        source = (device + FAR_LOW) * CELLS + place
                        if 0 <= source < NX:
                            columns[device, place, level * 8 + band * 4 + cell] = matrix[
                                device * CELLS + cell, source
                            ]
    down = np.zeros((GY * GZ, LEVELS, 2 * OWN, 256), ml_dtypes.bfloat16)
    up = np.zeros((GY * GZ, LEVELS, PADDED[2], 128), ml_dtypes.bfloat16)
    for level, pair in enumerate(chains(NY)):
        for device in range(GY * GZ):
            window = np.zeros((2, OWN, PADDED[level]))
            for place in range(SPAN[level]):
                source = device * OWN - LOW[level] + place
                if 0 <= source < NY:
                    for band in range(2):
                        window[band, :, place] = pair[band][
                            device * OWN : device * OWN + OWN, source
                        ]
            window = window.reshape(2 * OWN, PADDED[level])
            high, low = two_parts(window)
            down[device, level, :, : 3 * PADDED[level]] = np.concatenate([high, high, low], axis=1)
            up[device, level, : PADDED[level], : 6 * OWN] = np.concatenate([high, high, low]).T
    depth = np.zeros((LEVELS, 2, NZ, 2 * NZ), ml_dtypes.bfloat16)
    depth_back = np.zeros((LEVELS, 2, 2 * NZ, NZ), ml_dtypes.bfloat16)
    for level, pair in enumerate(chains(NZ)):
        both = np.concatenate(pair, axis=0)
        for part, value in enumerate(two_parts(both)):
            depth_back[level, part] = value
            depth[level, part] = value.T
    return columns, down, up, depth, depth_back


def segments(level):
    start, stop = -LOW[level], SPAN[level] - LOW[level]
    pieces = []
    for block in (-2, -1, 1, 2):
        low, high = max(start, block * OWN), min(stop, (block + 1) * OWN)
        if low < high:
            pieces.append((block, low - block * OWN, high - low, low - start))
    return pieces


def split(value):
    high = value.astype(jnp.bfloat16)
    return high, (value - high.astype(jnp.float32)).astype(jnp.bfloat16)


def stacked(value):
    high, low = split(value)
    return jnp.concatenate([high, low, high], axis=0)


def dot(a, b):
    return jnp.dot(a, b, preferred_element_type=jnp.float32)


def kernel(
    limits_hbm,
    volume_hbm,
    columns_hbm,
    down_hbm,
    up_hbm,
    depth_hbm,
    back_hbm,
    result,
    volume,
    limits,
    columns,
    down,
    up,
    depth,
    back,
    blocks,
    window0,
    window1,
    window2,
    spread0,
    spread1,
    spread2,
    landed,
    stacks,
    rows_in,
    bands,
    shrunk_high,
    shrunk_low,
    rows_out,
    terms,
    sums,
    finals,
    load_sem,
    first_send,
    first_recv,
    block_send,
    block_recv,
    row_send,
    row_recv,
    back_send,
    back_recv,
    sum_send,
    sum_recv,
    final_send,
    final_recv,
):
    gz, gy, gx = lax.axis_index("gz"), lax.axis_index("gy"), lax.axis_index("gx")
    pair, core = gy // 2, lax.rem(gy, 2)
    windows = (window0, window1, window2)
    spreads = (spread0, spread1, spread2)

    place = 4 * pair + 2 * gz + core
    at_home = gz == core

    def column_of(distance):
        return lax.rem(gx + distance + GX, GX)

    def column_peer(distance):
        return (gz, gy, column_of(distance))

    def worker(part, distance):
        return (core, 2 * pair + part, column_of(distance))

    def holder(half, distance):
        return (half, 2 * pair + gz, column_of(distance))

    def row_peer(block):
        other = lax.rem(place + block + 16, 16)
        return (lax.rem(other // 2, 2), 2 * (other // 4) + lax.rem(other, 2), gx)

    loads = [
        pltpu.make_async_copy(source, target, load_sem.at[index])
        for index, (source, target) in enumerate(
            (
                (volume_hbm, volume),
                (columns_hbm.at[gx], columns),
                (limits_hbm, limits),
                (down_hbm.at[place], down),
                (up_hbm.at[place], up),
                (depth_hbm, depth),
                (back_hbm, back),
            )
        )
    ]
    for load in loads:
        load.start()

    barrier = pltpu.get_barrier_semaphore()

    def greet(peer):
        pl.semaphore_signal(barrier, inc=1, device_id=peer, device_id_type=MESH)

    for part in range(2):
        for distance in (-7, 6, -1, 1):
            greet(worker(part, distance))
            greet(holder(part, -distance))
        pl.when(jnp.logical_not(jnp.logical_and(at_home, core == part)))(
            lambda part=part: greet(worker(part, 0))
        )
        pl.when(jnp.logical_not(jnp.logical_and(at_home, gz == part)))(
            lambda part=part: greet(holder(part, 0))
        )
    for distance in (-1, 1):
        greet(column_peer(distance))
    for block in (-2, -1, 1, 2):
        greet(row_peer(block))
    pl.semaphore_wait(barrier, 26 - 2 * at_home.astype(jnp.int32))

    ORDER = (0, -1, 1, 7, -6)

    def slot(d):
        return blocks.at[d - FAR_LOW]

    def depth_half(ref, half):
        if isinstance(half, int):
            return ref.at[:, :, half * HALF : (half + 1) * HALF]
        return ref.at[:, :, pl.ds(pl.multiple_of(half * HALF, HALF), HALF)]

    def first_copies(distance, part):
        target = -distance
        source = volume.at[:, part * OWN : (part + 1) * OWN]
        into = depth_half(slot(target), gz)
        index = ORDER.index(target)
        remote = pltpu.make_async_remote_copy(
            src_ref=source,
            dst_ref=into,
            send_sem=first_send.at[index, part],
            recv_sem=first_recv.at[index, gz],
            device_id=worker(part, distance),
            device_id_type=MESH,
        )
        return remote, source, into, first_recv.at[index, gz]

    def start_first(distance):
        for part in range(2):
            remote, source, into, recv = first_copies(distance, part)
            if distance == 0:
                here = jnp.logical_and(at_home, core == part)
                pl.when(jnp.logical_not(here))(remote.start)

                @pl.when(here)
                def _(source=source, into=into, recv=recv):
                    pltpu.make_async_copy(source, into, recv).start()

            else:
                remote.start()

    def wait_block(target):
        if target in ORDER:
            for half in range(2):
                into = depth_half(slot(target), half)
                recv = first_recv.at[ORDER.index(target), half]
                pltpu.make_async_copy(into, into, recv).wait()
        else:
            into = slot(target)
            pltpu.make_async_copy(into, into, block_recv.at[target - FAR_LOW]).wait()

    def wait_first_sent(distance):
        index = ORDER.index(-distance)
        for part in range(2):
            source = volume.at[:, part * OWN : (part + 1) * OWN]

            def wait(source=source, part=part):
                pltpu.make_async_copy(source, source, first_send.at[index, part]).wait()

            if distance == 0:
                pl.when(jnp.logical_not(jnp.logical_and(at_home, core == part)))(wait)
            else:
                wait()

    copies = []

    def pass_on(d, distance):
        target = d - distance
        copy = pltpu.make_async_remote_copy(
            src_ref=slot(d),
            dst_ref=slot(target),
            send_sem=block_send.at[target - FAR_LOW],
            recv_sem=block_recv.at[target - FAR_LOW],
            device_id=column_peer(distance),
            device_id_type=MESH,
        )
        copy.start()
        copies.append(copy)

    def take(d, distance=0):
        wait_block(d)
        if distance:
            pass_on(d, distance)

    def own_rows(level):
        return pl.ds(LOW[level], OWN)

    def add_block(d, fresh=False):
        source = slot(d)
        for level in range(LEVELS):
            if not REACH[level][0] <= d <= REACH[level][1]:
                continue

            def one(index, carry, level=level):
                total = None
                for cell in range(CELLS):
                    weight = columns[(d - FAR_LOW) * CELLS + cell, level * 8 + index]
                    term = weight * source[cell]
                    total = term if total is None else total + term
                if not fresh:
                    total = total + windows[level][index, own_rows(level)]
                windows[level][index, own_rows(level)] = total
                return carry

            lax.fori_loop(0, 8, one, 0)

    def row_copy(level, number, piece):
        block, first, count, into = piece
        return pltpu.make_async_remote_copy(
            src_ref=windows[level].at[:, pl.ds(LOW[level] + first, count)],
            dst_ref=windows[level].at[:, pl.ds(into, count)],
            send_sem=row_send.at[level, number],
            recv_sem=row_recv.at[level, number],
            device_id=row_peer(-block),
            device_id_type=MESH,
        )

    rows_sent = []

    def send_rows(level):
        for number, piece in enumerate(segments(level)):
            copy = row_copy(level, number, piece)
            copy.start()
            rows_sent.append((level, copy))

    def wait_rows(level):
        for owner, copy in rows_sent:
            if owner == level:
                copy.wait_recv()

    loads[0].wait()
    start_first(1)
    start_first(-1)
    start_first(0)
    wait_first_sent(1)
    wait_first_sent(-1)
    start_first(-7)
    start_first(6)
    loads[1].wait()
    take(-1, 1)
    take(1, -1)
    take(0)
    add_block(0, fresh=True)
    add_block(-1)
    add_block(1)
    send_rows(0)
    take(7, 1)
    take(-6, -1)
    add_block(7)
    add_block(-6)
    take(-2, 1)
    take(2, -1)
    add_block(-2)
    add_block(2)
    take(6, 1)
    take(-5)
    add_block(6)
    add_block(-5)
    take(-3, 1)
    take(3, -1)
    add_block(-3)
    add_block(3)
    send_rows(1)
    take(5)
    add_block(5)
    take(-4)
    add_block(-4)
    take(4)
    add_block(4)
    send_rows(2)

    for load in loads[2:]:
        load.wait()

    def shrink_level(level):
        span, padded = SPAN[level], PADDED[level]

        def rows_forth(index, carry):
            data = windows[level][index]
            if padded > span:
                data = jnp.concatenate(
                    [data, jnp.zeros((padded - span, NZ), jnp.float32)], axis=0
                )
            total = dot(down[level][:, : 3 * padded], stacked(data))
            rows_in[pl.ds(pl.multiple_of(index * 2 * OWN, 2 * OWN), 2 * OWN)] = total
            return carry

        lax.fori_loop(0, 8, rows_forth, 0, unroll=True)
        high, low = split(rows_in[...])
        bands[...] = (
            dot(high, depth[level, 0]) + dot(low, depth[level, 0]) + dot(high, depth[level, 1])
        )

        def shrink(index, carry):
            stack = index // 4
            for row_band in range(2):
                first = pl.multiple_of(index * 2 * OWN + row_band * OWN, OWN)
                for depth_band in range(2):
                    number = 4 * stack + 2 * row_band + depth_band
                    limit = limits[level, jnp.maximum(number - 1, 0)]
                    if row_band == 0 and depth_band == 0:
                        none = 0.0 if level == LEVELS - 1 else jnp.inf
                        limit = jnp.where(stack == 0, jnp.float32(none), limit)
                    spot = (pl.ds(first, OWN), pl.ds(depth_band * NZ, NZ))
                    value = bands[spot]
                    value = value - jnp.clip(value, -limit, limit)
                    shrunk_high[spot], shrunk_low[spot] = split(value)
            return carry

        lax.fori_loop(0, 8, shrink, 0, unroll=True)
        rows_out[...] = (
            dot(shrunk_high[...], back[level, 0])
            + dot(shrunk_low[...], back[level, 0])
            + dot(shrunk_high[...], back[level, 1])
        )

        def rows_back(index, carry):
            data = rows_out[pl.ds(pl.multiple_of(index * 2 * OWN, 2 * OWN), 2 * OWN)]
            total = dot(up[level][:padded, : 6 * OWN], stacked(data))
            spreads[level][index] = total[:span]
            return carry

        lax.fori_loop(0, 8, rows_back, 0, unroll=True)

    back_sent = []

    def send_back(level):
        for number, (block, _, count, into) in enumerate(segments(level)):
            copy = pltpu.make_async_remote_copy(
                src_ref=spreads[level].at[:, pl.ds(into, count)],
                dst_ref=landed.at[level, number, :, pl.ds(0, count)],
                send_sem=back_send.at[level, number],
                recv_sem=back_recv.at[level, number],
                device_id=row_peer(block),
                device_id_type=MESH,
            )
            copy.start()
            back_sent.append((level, copy))

    def gather_back(level):
        for owner, copy in back_sent:
            if owner == level:
                copy.wait_recv()

        def one(index, carry):
            for group in range(OWN // 8):
                total = spreads[level][index, pl.ds(LOW[level] + group * 8, 8)]
                for number, (_, first, count, _) in enumerate(segments(level)):
                    if first <= group * 8 < first + count:
                        total = total + landed[level, number, index, pl.ds(group * 8 - first, 8)]
                stacks[level, index, pl.ds(group * 8, 8)] = total
            return carry

        lax.fori_loop(0, 8, one, 0)

    wait_rows(0)
    shrink_level(0)
    send_back(0)
    wait_rows(1)
    shrink_level(1)
    send_back(1)
    wait_rows(2)
    shrink_level(2)
    send_back(2)
    gather_back(2)

    def term(d):
        return terms.at[d - FAR_LOW]

    def fill(d):
        target = term(d)

        def one(cell, carry):
            total = None
            for level in range(LEVELS):
                if not REACH[level][0] <= d <= REACH[level][1]:
                    continue
                for index in range(8):
                    weight = columns[(d - FAR_LOW) * CELLS + cell, level * 8 + index]
                    product = weight * stacks[level, index]
                    total = product if total is None else total + product
            target[cell] = total
            return carry

        lax.fori_loop(0, CELLS, one, 0)

    UP3, UP2, UP1, DN3, DN2, DN1, HI6, HI7, LO6 = range(9)
    SAME, UP0, DN0, HI0, LO0 = range(5)
    moved = []

    def hand_on(source, target, distance):
        copy = pltpu.make_async_remote_copy(
            src_ref=source,
            dst_ref=sums.at[target],
            send_sem=sum_send.at[target],
            recv_sem=sum_recv.at[target],
            device_id=column_peer(distance),
            device_id_type=MESH,
        )
        copy.start()
        moved.append(copy)
        return copy

    def add_term(which, d):
        spot = sums.at[which]
        pltpu.make_async_copy(spot, spot, sum_recv.at[which]).wait()
        spot[...] = spot[...] + term(d)[...]
        return spot

    def deliver(source, which, distance):
        into = finals.at[which, :, pl.ds(pl.multiple_of(core * OWN, OWN), OWN)]
        for half in range(2):
            part = depth_half(source, half)
            remote = pltpu.make_async_remote_copy(
                src_ref=part,
                dst_ref=into,
                send_sem=final_send.at[which, half],
                recv_sem=final_recv.at[which, core],
                device_id=holder(half, distance),
                device_id_type=MESH,
            )
            if which == SAME:
                here = jnp.logical_and(at_home, gz == half)
                pl.when(jnp.logical_not(here))(remote.start)

                @pl.when(here)
                def _(part=part):
                    pltpu.make_async_copy(part, into, final_recv.at[which, core]).start()

            else:
                remote.start()

    def wait_delivered(which):
        for half in range(2):
            part = depth_half(term(0), half)

            def wait(part=part, half=half):
                pltpu.make_async_copy(part, part, final_send.at[which, half]).wait()

            if which == SAME:
                pl.when(jnp.logical_not(jnp.logical_and(at_home, gz == half)))(wait)
            else:
                wait()

    fill(4)
    first = hand_on(term(4), UP3, 1)
    fill(-4)
    second = hand_on(term(-4), DN3, -1)
    fill(5)
    fill(-5)
    first.wait_send()
    second.wait_send()
    moved.clear()
    hand_on(term(5), HI6, -1)
    hand_on(term(-5), LO6, 1)
    gather_back(1)
    fill(3)
    fill(-3)
    hand_on(add_term(UP3, 3), UP2, 1)
    hand_on(add_term(DN3, -3), DN2, -1)
    fill(6)
    fill(-6)
    hand_on(add_term(HI6, 6), HI7, -1)
    deliver(add_term(LO6, -6), LO0, -6)
    fill(2)
    fill(-2)
    hand_on(add_term(UP2, 2), UP1, 1)
    hand_on(add_term(DN2, -2), DN1, -1)
    fill(7)
    deliver(add_term(HI7, 7), HI0, 7)
    gather_back(0)
    fill(0)
    deliver(term(0), SAME, 0)
    fill(1)
    fill(-1)
    deliver(add_term(UP1, 1), UP0, 1)
    deliver(add_term(DN1, -1), DN0, -1)
    total = None
    for which in (LO0, SAME, HI0, UP0, DN0):
        for part in range(2):
            spot = finals.at[which, :, pl.ds(part * OWN, OWN)]
            pltpu.make_async_copy(spot, spot, final_recv.at[which, part]).wait()
        total = finals[which] if total is None else total + finals[which]
    result[...] = total

    for distance in (0, -7, 6):
        wait_first_sent(distance)
    for copy in copies:
        copy.wait_send()
    for _, copy in rows_sent + back_sent:
        copy.wait_send()
    for copy in moved:
        copy.wait_send()
    for which in range(5):
        wait_delivered(which)


def per_device(volume, thresholds):
    columns, down, up, depth, back = tables()
    block = (CELLS, OWN, NZ)
    f32, bf16 = jnp.float32, jnp.bfloat16
    vmem, dma = pltpu.VMEM, pltpu.SemaphoreType.DMA
    window_shapes = [vmem((8, span, NZ), f32) for span in SPAN]
    count = FAR_HIGH - FAR_LOW + 1
    return pl.pallas_call(
        kernel,
        out_shape=pltpu.VMEM(volume.shape, volume.dtype),
        in_specs=[pl.BlockSpec(memory_space=pltpu.HBM)] * 7,
        out_specs=pl.BlockSpec(memory_space=pltpu.VMEM),
        scratch_shapes=[
            vmem(volume.shape, f32),
            pltpu.SMEM(thresholds.shape, f32),
            pltpu.SMEM(columns.shape[1:], f32),
            vmem(down.shape[1:], bf16),
            vmem(up.shape[1:], bf16),
            vmem(depth.shape, bf16),
            vmem(back.shape, bf16),
            vmem((count,) + block, f32),
            *window_shapes,
            *window_shapes,
            vmem((LEVELS, 4, 8, OWN, NZ), f32),
            vmem((LEVELS, 8, OWN, NZ), f32),
            vmem((16 * OWN, NZ), f32),
            vmem((16 * OWN, 2 * NZ), f32),
            vmem((16 * OWN, 2 * NZ), bf16),
            vmem((16 * OWN, 2 * NZ), bf16),
            vmem((16 * OWN, NZ), f32),
            vmem((count,) + block, f32),
            vmem((9,) + block, f32),
            vmem((5,) + volume.shape, f32),
            dma((7,)),
            dma((5, 2)),
            dma((5, 2)),
            dma((count,)),
            dma((count,)),
            dma((LEVELS, 4)),
            dma((LEVELS, 4)),
            dma((LEVELS, 4)),
            dma((LEVELS, 4)),
            dma((9,)),
            dma((9,)),
            dma((5, 2)),
            dma((5, 2)),
        ],
        compiler_params=pltpu.CompilerParams(
            collective_id=0, has_side_effects=True, vmem_limit_bytes=60 * 2**20
        ),
        name="shrinkage",
    )(thresholds, volume, columns, down, up, depth, back)


def solution(mesh):
    placed = (P("gx", "gy", "gz"), P())
    return jax.shard_map(
        per_device, mesh=mesh, in_specs=placed, out_specs=P("gx", "gy", "gz"), check_vma=False
    )
```

```python
import math

import jax
import jax.numpy as jnp
import ml_dtypes
import numpy as np
from jax import lax
from jax.experimental import pallas as pl
from jax.experimental.pallas import tpu as pltpu
from jax.sharding import PartitionSpec as P

MESH = pl.DeviceIdType.MESH
LEVELS = 3
NX, NY, NZ = 128, 256, 256
GX, GY, GZ = 32, 8, 2
CELLS = NX // GX
ROWS = NY // GY
HALF = NZ // GZ
OWN = ROWS // GZ

base_taps = [
    0.23037781330885523,
    0.7148465705525415,
    0.6308807679295904,
    -0.02798376941698385,
    -0.18703481171888114,
    0.030841381835986965,
    0.032883011666982945,
    -0.010597401784997278,
]
scaling_taps = [value / math.sqrt(2.0) for value in base_taps]
wavelet_taps = [(-1.0) ** index * base_taps[7 - index] / math.sqrt(2.0) for index in range(8)]

FAR_LOW, FAR_HIGH = -6, 7
REACH = ((-1, 1), (-3, 3), (FAR_LOW, FAR_HIGH))
LOW = (8, 16, 24)
SPAN = (32, 48, 72)
PADDED = (32, 48, 80)


def chains(count):
    def banded(taps, step):
        out = np.zeros((count, count))
        for index, tap in enumerate(taps):
            offset = (index - 3) * step
            rows = np.arange(max(0, -offset), min(count, count - offset))
            out[rows, rows + offset] = tap
        return out

    so_far, result = np.eye(count), []
    for level in range(LEVELS):
        low = banded(scaling_taps, 2**level) @ so_far
        high = banded(wavelet_taps, 2**level) @ so_far
        result.append((low, high))
        so_far = low
    return result


def two_parts(table):
    high = table.astype(ml_dtypes.bfloat16)
    low = (table - high.astype(np.float64)).astype(ml_dtypes.bfloat16)
    return high, low


def tables():
    columns = np.zeros((GX, (FAR_HIGH - FAR_LOW + 1) * CELLS, 128), np.float32)
    for level, pair in enumerate(chains(NX)):
        for band, matrix in enumerate(pair):
            for device in range(GX):
                for cell in range(CELLS):
                    for place in range(columns.shape[1]):
                        source = (device + FAR_LOW) * CELLS + place
                        if 0 <= source < NX:
                            columns[device, place, level * 8 + band * 4 + cell] = matrix[
                                device * CELLS + cell, source
                            ]
    down = np.zeros((GY * GZ, LEVELS, 2 * OWN, 256), ml_dtypes.bfloat16)
    up = np.zeros((GY * GZ, LEVELS, PADDED[2], 128), ml_dtypes.bfloat16)
    for level, pair in enumerate(chains(NY)):
        for device in range(GY * GZ):
            window = np.zeros((2, OWN, PADDED[level]))
            for place in range(SPAN[level]):
                source = device * OWN - LOW[level] + place
                if 0 <= source < NY:
                    for band in range(2):
                        window[band, :, place] = pair[band][
                            device * OWN : device * OWN + OWN, source
                        ]
            window = window.reshape(2 * OWN, PADDED[level])
            high, low = two_parts(window)
            down[device, level, :, : 3 * PADDED[level]] = np.concatenate([high, high, low], axis=1)
            up[device, level, : PADDED[level], : 6 * OWN] = np.concatenate([high, high, low]).T
    depth = np.zeros((LEVELS, 2, NZ, 2 * NZ), ml_dtypes.bfloat16)
    depth_back = np.zeros((LEVELS, 2, 2 * NZ, NZ), ml_dtypes.bfloat16)
    for level, pair in enumerate(chains(NZ)):
        both = np.concatenate(pair, axis=0)
        for part, value in enumerate(two_parts(both)):
            depth_back[level, part] = value
            depth[level, part] = value.T
    return columns, down, up, depth, depth_back


def segments(level):
    start, stop = -LOW[level], SPAN[level] - LOW[level]
    pieces = []
    for block in (-2, -1, 1, 2):
        low, high = max(start, block * OWN), min(stop, (block + 1) * OWN)
        if low < high:
            pieces.append((block, low - block * OWN, high - low, low - start))
    return pieces


def split(value):
    high = value.astype(jnp.bfloat16)
    return high, (value - high.astype(jnp.float32)).astype(jnp.bfloat16)


def stacked(value):
    high, low = split(value)
    return jnp.concatenate([high, low, high], axis=0)


def dot(a, b):
    return jnp.dot(a, b, preferred_element_type=jnp.float32)


def kernel(
    limits_hbm,
    volume_hbm,
    columns_hbm,
    down_hbm,
    up_hbm,
    depth_hbm,
    back_hbm,
    result,
    volume,
    limits,
    columns,
    down,
    up,
    depth,
    back,
    blocks,
    window0,
    window1,
    window2,
    spread0,
    spread1,
    spread2,
    landed,
    stacks,
    rows_in,
    bands,
    shrunk_high,
    shrunk_low,
    rows_out,
    terms,
    sums,
    finals,
    load_sem,
    first_send,
    first_recv,
    block_send,
    block_recv,
    row_send,
    row_recv,
    back_send,
    back_recv,
    sum_send,
    sum_recv,
    final_send,
    final_recv,
):
    gz, gy, gx = lax.axis_index("gz"), lax.axis_index("gy"), lax.axis_index("gx")
    pair, core = gy // 2, lax.rem(gy, 2)
    windows = (window0, window1, window2)
    spreads = (spread0, spread1, spread2)

    place = 4 * pair + 2 * gz + core
    at_home = gz == core

    def column_of(distance):
        return lax.rem(gx + distance + GX, GX)

    def column_peer(distance):
        return (gz, gy, column_of(distance))

    def worker(part, distance):
        return (core, 2 * pair + part, column_of(distance))

    def holder(half, distance):
        return (half, 2 * pair + gz, column_of(distance))

    def row_peer(block):
        other = lax.rem(place + block + 16, 16)
        return (lax.rem(other // 2, 2), 2 * (other // 4) + lax.rem(other, 2), gx)

    loads = [
        pltpu.make_async_copy(source, target, load_sem.at[index])
        for index, (source, target) in enumerate(
            (
                (volume_hbm, volume),
                (columns_hbm.at[gx], columns),
                (limits_hbm, limits),
                (down_hbm.at[place], down),
                (up_hbm.at[place], up),
                (depth_hbm, depth),
                (back_hbm, back),
            )
        )
    ]
    for load in loads:
        load.start()

    barrier = pltpu.get_barrier_semaphore()

    def greet(peer):
        pl.semaphore_signal(barrier, inc=1, device_id=peer, device_id_type=MESH)

    for part in range(2):
        for distance in (-1, 1):
            greet(worker(part, distance))
            greet(holder(part, distance))
        pl.when(jnp.logical_not(jnp.logical_and(at_home, core == part)))(
            lambda part=part: greet(worker(part, 0))
        )
        pl.when(jnp.logical_not(jnp.logical_and(at_home, gz == part)))(
            lambda part=part: greet(holder(part, 0))
        )
    for distance in (-8, -1, 1, 8):
        greet(column_peer(distance))
    for block in (-2, -1, 1, 2):
        greet(row_peer(block))
    pl.semaphore_wait(barrier, 20 - 2 * at_home.astype(jnp.int32))

    ORDER = (0, -1, 1)

    def slot(d):
        return blocks.at[d - FAR_LOW]

    def depth_half(ref, half):
        if isinstance(half, int):
            return ref.at[:, :, half * HALF : (half + 1) * HALF]
        return ref.at[:, :, pl.ds(pl.multiple_of(half * HALF, HALF), HALF)]

    def first_copies(distance, part):
        target = -distance
        source = volume.at[:, part * OWN : (part + 1) * OWN]
        into = depth_half(slot(target), gz)
        index = ORDER.index(target)
        remote = pltpu.make_async_remote_copy(
            src_ref=source,
            dst_ref=into,
            send_sem=first_send.at[index, part],
            recv_sem=first_recv.at[index, gz],
            device_id=worker(part, distance),
            device_id_type=MESH,
        )
        return remote, source, into, first_recv.at[index, gz]

    def start_first(distance):
        for part in range(2):
            remote, source, into, recv = first_copies(distance, part)
            if distance == 0:
                here = jnp.logical_and(at_home, core == part)
                pl.when(jnp.logical_not(here))(remote.start)

                @pl.when(here)
                def _(source=source, into=into, recv=recv):
                    pltpu.make_async_copy(source, into, recv).start()

            else:
                remote.start()

    def wait_block(target):
        if target in ORDER:
            for half in range(2):
                into = depth_half(slot(target), half)
                recv = first_recv.at[ORDER.index(target), half]
                pltpu.make_async_copy(into, into, recv).wait()
        else:
            into = slot(target)
            pltpu.make_async_copy(into, into, block_recv.at[target - FAR_LOW]).wait()

    def wait_first_sent(distance):
        index = ORDER.index(-distance)
        for part in range(2):
            source = volume.at[:, part * OWN : (part + 1) * OWN]

            def wait(source=source, part=part):
                pltpu.make_async_copy(source, source, first_send.at[index, part]).wait()

            if distance == 0:
                pl.when(jnp.logical_not(jnp.logical_and(at_home, core == part)))(wait)
            else:
                wait()

    copies = []

    def pass_on(d, distance):
        target = d - distance
        copy = pltpu.make_async_remote_copy(
            src_ref=slot(d),
            dst_ref=slot(target),
            send_sem=block_send.at[target - FAR_LOW],
            recv_sem=block_recv.at[target - FAR_LOW],
            device_id=column_peer(distance),
            device_id_type=MESH,
        )
        copy.start()
        copies.append(copy)

    def take(d, *distances):
        wait_block(d)
        for distance in distances:
            pass_on(d, distance)

    def own_rows(level):
        return pl.ds(LOW[level], OWN)

    def add_block(d, fresh=False):
        source = slot(d)
        for level in range(LEVELS):
            if not REACH[level][0] <= d <= REACH[level][1]:
                continue

            def one(index, carry, level=level):
                total = None
                for cell in range(CELLS):
                    weight = columns[(d - FAR_LOW) * CELLS + cell, level * 8 + index]
                    term = weight * source[cell]
                    total = term if total is None else total + term
                if not fresh:
                    total = total + windows[level][index, own_rows(level)]
                windows[level][index, own_rows(level)] = total
                return carry

            lax.fori_loop(0, 8, one, 0)

    def row_copy(level, number, piece):
        block, first, count, into = piece
        return pltpu.make_async_remote_copy(
            src_ref=windows[level].at[:, pl.ds(LOW[level] + first, count)],
            dst_ref=windows[level].at[:, pl.ds(into, count)],
            send_sem=row_send.at[level, number],
            recv_sem=row_recv.at[level, number],
            device_id=row_peer(-block),
            device_id_type=MESH,
        )

    rows_sent = []

    def send_rows(level):
        for number, piece in enumerate(segments(level)):
            copy = row_copy(level, number, piece)
            copy.start()
            rows_sent.append((level, copy))

    def wait_rows(level):
        for owner, copy in rows_sent:
            if owner == level:
                copy.wait_recv()

    loads[0].wait()
    start_first(1)
    start_first(-1)
    start_first(0)
    loads[1].wait()
    take(-1, 1, -8)
    take(1, -1)
    take(0)
    add_block(0, fresh=True)
    add_block(-1)
    add_block(1)
    send_rows(0)
    take(-2, 1, -8)
    take(2, -1, 8)
    add_block(-2)
    add_block(2)
    take(7)
    add_block(7)
    take(-3, 1, -8)
    take(3, -1, 8)
    add_block(-3)
    add_block(3)
    send_rows(1)
    take(6)
    add_block(6)
    take(-6)
    add_block(-6)
    take(-4)
    add_block(-4)
    take(4)
    add_block(4)
    take(5)
    add_block(5)
    take(-5)
    add_block(-5)
    send_rows(2)

    for load in loads[2:]:
        load.wait()

    def shrink_level(level):
        span, padded = SPAN[level], PADDED[level]

        def rows_forth(index, carry):
            data = windows[level][index]
            if padded > span:
                data = jnp.concatenate(
                    [data, jnp.zeros((padded - span, NZ), jnp.float32)], axis=0
                )
            total = dot(down[level][:, : 3 * padded], stacked(data))
            rows_in[pl.ds(pl.multiple_of(index * 2 * OWN, 2 * OWN), 2 * OWN)] = total
            return carry

        lax.fori_loop(0, 8, rows_forth, 0, unroll=True)
        high, low = split(rows_in[...])
        bands[...] = (
            dot(high, depth[level, 0]) + dot(low, depth[level, 0]) + dot(high, depth[level, 1])
        )

        def shrink(index, carry):
            stack = index // 4
            for row_band in range(2):
                first = pl.multiple_of(index * 2 * OWN + row_band * OWN, OWN)
                for depth_band in range(2):
                    number = 4 * stack + 2 * row_band + depth_band
                    limit = limits[level, jnp.maximum(number - 1, 0)]
                    if row_band == 0 and depth_band == 0:
                        none = 0.0 if level == LEVELS - 1 else jnp.inf
                        limit = jnp.where(stack == 0, jnp.float32(none), limit)
                    spot = (pl.ds(first, OWN), pl.ds(depth_band * NZ, NZ))
                    value = bands[spot]
                    value = value - jnp.clip(value, -limit, limit)
                    shrunk_high[spot], shrunk_low[spot] = split(value)
            return carry

        lax.fori_loop(0, 8, shrink, 0, unroll=True)
        rows_out[...] = (
            dot(shrunk_high[...], back[level, 0])
            + dot(shrunk_low[...], back[level, 0])
            + dot(shrunk_high[...], back[level, 1])
        )

        def rows_back(index, carry):
            data = rows_out[pl.ds(pl.multiple_of(index * 2 * OWN, 2 * OWN), 2 * OWN)]
            total = dot(up[level][:padded, : 6 * OWN], stacked(data))
            spreads[level][index] = total[:span]
            return carry

        lax.fori_loop(0, 8, rows_back, 0, unroll=True)

    back_sent = []

    def send_back(level):
        for number, (block, _, count, into) in enumerate(segments(level)):
            copy = pltpu.make_async_remote_copy(
                src_ref=spreads[level].at[:, pl.ds(into, count)],
                dst_ref=landed.at[level, number, :, pl.ds(0, count)],
                send_sem=back_send.at[level, number],
                recv_sem=back_recv.at[level, number],
                device_id=row_peer(block),
                device_id_type=MESH,
            )
            copy.start()
            back_sent.append((level, copy))

    def gather_back(level):
        for owner, copy in back_sent:
            if owner == level:
                copy.wait_recv()

        def one(index, carry):
            for group in range(OWN // 8):
                total = spreads[level][index, pl.ds(LOW[level] + group * 8, 8)]
                for number, (_, first, count, _) in enumerate(segments(level)):
                    if first <= group * 8 < first + count:
                        total = total + landed[level, number, index, pl.ds(group * 8 - first, 8)]
                stacks[level, index, pl.ds(group * 8, 8)] = total
            return carry

        lax.fori_loop(0, 8, one, 0)

    wait_rows(0)
    shrink_level(0)
    send_back(0)
    wait_rows(1)
    shrink_level(1)
    send_back(1)
    wait_rows(2)
    shrink_level(2)
    send_back(2)
    gather_back(2)

    def term(d):
        return terms.at[d - FAR_LOW]

    def fill(d):
        target = term(d)

        def one(cell, carry):
            total = None
            for level in range(LEVELS):
                if not REACH[level][0] <= d <= REACH[level][1]:
                    continue
                for index in range(8):
                    weight = columns[(d - FAR_LOW) * CELLS + cell, level * 8 + index]
                    product = weight * stacks[level, index]
                    total = product if total is None else total + product
            target[cell] = total
            return carry

        lax.fori_loop(0, CELLS, one, 0)

    UP3, UP2, UP1, DN3, DN2, DN1, HI5, HI6, HI7, LO5, LO6 = range(11)
    SAME, UP0, DN0 = range(3)
    moved = []

    def hand_on(source, target, distance):
        copy = pltpu.make_async_remote_copy(
            src_ref=source,
            dst_ref=sums.at[target],
            send_sem=sum_send.at[target],
            recv_sem=sum_recv.at[target],
            device_id=column_peer(distance),
            device_id_type=MESH,
        )
        copy.start()
        moved.append(copy)
        return copy

    def arrived(which):
        spot = sums.at[which]
        pltpu.make_async_copy(spot, spot, sum_recv.at[which]).wait()
        return spot

    def join(d, which):
        term(d)[...] = term(d)[...] + arrived(which)[...]

    def add_term(which, d):
        spot = arrived(which)
        spot[...] = spot[...] + term(d)[...]
        return spot

    def deliver(source, which, distance):
        into = finals.at[which, :, pl.ds(pl.multiple_of(core * OWN, OWN), OWN)]
        for half in range(2):
            part = depth_half(source, half)
            remote = pltpu.make_async_remote_copy(
                src_ref=part,
                dst_ref=into,
                send_sem=final_send.at[which, half],
                recv_sem=final_recv.at[which, core],
                device_id=holder(half, distance),
                device_id_type=MESH,
            )
            if which == SAME:
                here = jnp.logical_and(at_home, gz == half)
                pl.when(jnp.logical_not(here))(remote.start)

                @pl.when(here)
                def _(part=part):
                    pltpu.make_async_copy(part, into, final_recv.at[which, core]).start()

            else:
                remote.start()

    def wait_delivered(which):
        for half in range(2):
            part = depth_half(term(0), half)

            def wait(part=part, half=half):
                pltpu.make_async_copy(part, part, final_send.at[which, half]).wait()

            if which == SAME:
                pl.when(jnp.logical_not(jnp.logical_and(at_home, gz == half)))(wait)
            else:
                wait()

    for d, target, distance in (
        (4, UP3, 1),
        (-4, DN3, -1),
        (5, HI5, 8),
        (-5, LO5, -8),
        (6, HI6, 8),
        (-6, LO6, -8),
        (7, HI7, 8),
    ):
        fill(d)
        hand_on(term(d), target, distance)
    gather_back(1)
    fill(3)
    fill(-3)
    join(3, LO5)
    join(-3, HI5)
    hand_on(add_term(UP3, 3), UP2, 1)
    hand_on(add_term(DN3, -3), DN2, -1)
    fill(2)
    fill(-2)
    join(2, LO6)
    join(-2, HI6)
    hand_on(add_term(UP2, 2), UP1, 1)
    hand_on(add_term(DN2, -2), DN1, -1)
    gather_back(0)
    fill(0)
    deliver(term(0), SAME, 0)
    fill(1)
    fill(-1)
    join(-1, HI7)
    deliver(add_term(UP1, 1), UP0, 1)
    deliver(add_term(DN1, -1), DN0, -1)
    total = None
    for which in (SAME, UP0, DN0):
        for part in range(2):
            spot = finals.at[which, :, pl.ds(part * OWN, OWN)]
            pltpu.make_async_copy(spot, spot, final_recv.at[which, part]).wait()
        total = finals[which] if total is None else total + finals[which]
    result[...] = total

    for distance in (-1, 0, 1):
        wait_first_sent(distance)
    for copy in copies:
        copy.wait_send()
    for _, copy in rows_sent + back_sent:
        copy.wait_send()
    for copy in moved:
        copy.wait_send()
    for which in range(3):
        wait_delivered(which)


def per_device(volume, thresholds):
    columns, down, up, depth, back = tables()
    block = (CELLS, OWN, NZ)
    f32, bf16 = jnp.float32, jnp.bfloat16
    vmem, dma = pltpu.VMEM, pltpu.SemaphoreType.DMA
    window_shapes = [vmem((8, span, NZ), f32) for span in SPAN]
    count = FAR_HIGH - FAR_LOW + 1
    return pl.pallas_call(
        kernel,
        out_shape=pltpu.VMEM(volume.shape, volume.dtype),
        in_specs=[pl.BlockSpec(memory_space=pltpu.HBM)] * 7,
        out_specs=pl.BlockSpec(memory_space=pltpu.VMEM),
        scratch_shapes=[
            vmem(volume.shape, f32),
            pltpu.SMEM(thresholds.shape, f32),
            pltpu.SMEM(columns.shape[1:], f32),
            vmem(down.shape[1:], bf16),
            vmem(up.shape[1:], bf16),
            vmem(depth.shape, bf16),
            vmem(back.shape, bf16),
            vmem((count,) + block, f32),
            *window_shapes,
            *window_shapes,
            vmem((LEVELS, 4, 8, OWN, NZ), f32),
            vmem((LEVELS, 8, OWN, NZ), f32),
            vmem((16 * OWN, NZ), f32),
            vmem((16 * OWN, 2 * NZ), f32),
            vmem((16 * OWN, 2 * NZ), bf16),
            vmem((16 * OWN, 2 * NZ), bf16),
            vmem((16 * OWN, NZ), f32),
            vmem((count,) + block, f32),
            vmem((11,) + block, f32),
            vmem((3,) + volume.shape, f32),
            dma((7,)),
            dma((3, 2)),
            dma((3, 2)),
            dma((count,)),
            dma((count,)),
            dma((LEVELS, 4)),
            dma((LEVELS, 4)),
            dma((LEVELS, 4)),
            dma((LEVELS, 4)),
            dma((11,)),
            dma((11,)),
            dma((3, 2)),
            dma((3, 2)),
        ],
        compiler_params=pltpu.CompilerParams(
            collective_id=0, has_side_effects=True, vmem_limit_bytes=60 * 2**20
        ),
        name="shrinkage",
    )(thresholds, volume, columns, down, up, depth, back)


def solution(mesh):
    placed = (P("gx", "gy", "gz"), P())
    return jax.shard_map(
        per_device, mesh=mesh, in_specs=placed, out_specs=P("gx", "gy", "gz"), check_vma=False
    )
```

```python
import math

import jax
import jax.numpy as jnp
import ml_dtypes
import numpy as np
from jax import lax
from jax.experimental import pallas as pl
from jax.experimental.pallas import tpu as pltpu
from jax.sharding import PartitionSpec as P

MESH = pl.DeviceIdType.MESH
LEVELS = 3
NX, NY, NZ = 128, 256, 256
GX, GY, GZ = 32, 8, 2
CELLS = NX // GX
ROWS = NY // GY
HALF = NZ // GZ
OWN = ROWS // GZ

base_taps = [
    0.23037781330885523,
    0.7148465705525415,
    0.6308807679295904,
    -0.02798376941698385,
    -0.18703481171888114,
    0.030841381835986965,
    0.032883011666982945,
    -0.010597401784997278,
]
scaling_taps = [value / math.sqrt(2.0) for value in base_taps]
wavelet_taps = [(-1.0) ** index * base_taps[7 - index] / math.sqrt(2.0) for index in range(8)]

FAR_LOW, FAR_HIGH = -6, 7
REACH = ((-1, 1), (-3, 3), (FAR_LOW, FAR_HIGH))
LOW = (8, 16, 24)
SPAN = (32, 48, 72)
PADDED = (32, 48, 80)
PARTS = ((slice(0, 8),), (slice(0, 8),), (slice(0, 4), slice(4, 8)))


def chains(count):
    def banded(taps, step):
        out = np.zeros((count, count))
        for index, tap in enumerate(taps):
            offset = (index - 3) * step
            rows = np.arange(max(0, -offset), min(count, count - offset))
            out[rows, rows + offset] = tap
        return out

    so_far, result = np.eye(count), []
    for level in range(LEVELS):
        low = banded(scaling_taps, 2**level) @ so_far
        high = banded(wavelet_taps, 2**level) @ so_far
        result.append((low, high))
        so_far = low
    return result


def two_parts(table):
    high = table.astype(ml_dtypes.bfloat16)
    low = (table - high.astype(np.float64)).astype(ml_dtypes.bfloat16)
    return high, low


def tables():
    columns = np.zeros((GX, (FAR_HIGH - FAR_LOW + 1) * CELLS, 128), np.float32)
    for level, pair in enumerate(chains(NX)):
        for band, matrix in enumerate(pair):
            for device in range(GX):
                for cell in range(CELLS):
                    for place in range(columns.shape[1]):
                        source = (device + FAR_LOW) * CELLS + place
                        if 0 <= source < NX:
                            columns[device, place, level * 8 + band * 4 + cell] = matrix[
                                device * CELLS + cell, source
                            ]
    down = np.zeros((GY * GZ, LEVELS, 2 * OWN, 256), ml_dtypes.bfloat16)
    up = np.zeros((GY * GZ, LEVELS, PADDED[2], 128), ml_dtypes.bfloat16)
    for level, pair in enumerate(chains(NY)):
        for device in range(GY * GZ):
            window = np.zeros((2, OWN, PADDED[level]))
            for place in range(SPAN[level]):
                source = device * OWN - LOW[level] + place
                if 0 <= source < NY:
                    for band in range(2):
                        window[band, :, place] = pair[band][
                            device * OWN : device * OWN + OWN, source
                        ]
            window = window.reshape(2 * OWN, PADDED[level])
            high, low = two_parts(window)
            down[device, level, :, : 3 * PADDED[level]] = np.concatenate([high, high, low], axis=1)
            up[device, level, : PADDED[level], : 6 * OWN] = np.concatenate([high, high, low]).T
    depth = np.zeros((LEVELS, 2, NZ, 2 * NZ), ml_dtypes.bfloat16)
    depth_back = np.zeros((LEVELS, 2, 2 * NZ, NZ), ml_dtypes.bfloat16)
    for level, pair in enumerate(chains(NZ)):
        both = np.concatenate(pair, axis=0)
        for part, value in enumerate(two_parts(both)):
            depth_back[level, part] = value
            depth[level, part] = value.T
    return columns, down, up, depth, depth_back


def segments(level):
    start, stop = -LOW[level], SPAN[level] - LOW[level]
    pieces = []
    for block in (-2, -1, 1, 2):
        low, high = max(start, block * OWN), min(stop, (block + 1) * OWN)
        if low < high:
            pieces.append((block, low - block * OWN, high - low, low - start))
    return pieces


def split(value):
    high = value.astype(jnp.bfloat16)
    return high, (value - high.astype(jnp.float32)).astype(jnp.bfloat16)


def stacked(value):
    high, low = split(value)
    return jnp.concatenate([high, low, high], axis=0)


def dot(a, b):
    return jnp.dot(a, b, preferred_element_type=jnp.float32)


def kernel(
    limits_hbm,
    volume_hbm,
    columns_hbm,
    down_hbm,
    up_hbm,
    depth_hbm,
    back_hbm,
    result,
    volume,
    limits,
    columns,
    down,
    up,
    depth,
    back,
    blocks,
    window0,
    window1,
    window2,
    spread0,
    spread1,
    spread2,
    landed,
    stacks,
    rows_in,
    bands,
    shrunk_high,
    shrunk_low,
    rows_out,
    terms,
    sums,
    finals,
    load_sem,
    first_send,
    first_recv,
    block_send,
    block_recv,
    row_send,
    row_recv,
    back_send,
    back_recv,
    sum_send,
    sum_recv,
    final_send,
    final_recv,
):
    gz, gy, gx = lax.axis_index("gz"), lax.axis_index("gy"), lax.axis_index("gx")
    pair, core = gy // 2, lax.rem(gy, 2)
    windows = (window0, window1, window2)
    spreads = (spread0, spread1, spread2)

    place = 4 * pair + 2 * gz + core
    at_home = gz == core

    def column_of(distance):
        return lax.rem(gx + distance + GX, GX)

    def column_peer(distance):
        return (gz, gy, column_of(distance))

    def worker(part, distance):
        return (core, 2 * pair + part, column_of(distance))

    def holder(half, distance):
        return (half, 2 * pair + gz, column_of(distance))

    def row_peer(block):
        other = lax.rem(place + block + 16, 16)
        return (lax.rem(other // 2, 2), 2 * (other // 4) + lax.rem(other, 2), gx)

    loads = [
        pltpu.make_async_copy(source, target, load_sem.at[index])
        for index, (source, target) in enumerate(
            (
                (volume_hbm, volume),
                (columns_hbm.at[gx], columns),
                (limits_hbm, limits),
                (down_hbm.at[place], down),
                (up_hbm.at[place], up),
                (depth_hbm, depth),
                (back_hbm, back),
            )
        )
    ]
    loads[0].start()

    barrier = pltpu.get_barrier_semaphore()

    def greet(peer):
        pl.semaphore_signal(barrier, inc=1, device_id=peer, device_id_type=MESH)

    for part in range(2):
        for distance in (-1, 1):
            greet(worker(part, distance))
            greet(holder(part, distance))
        pl.when(jnp.logical_not(jnp.logical_and(at_home, core == part)))(
            lambda part=part: greet(worker(part, 0))
        )
        pl.when(jnp.logical_not(jnp.logical_and(at_home, gz == part)))(
            lambda part=part: greet(holder(part, 0))
        )
    for distance in (-8, -1, 1, 8):
        greet(column_peer(distance))
    for block in (-2, -1, 1, 2):
        greet(row_peer(block))
    for load in loads[1:]:
        load.start()
    pl.semaphore_wait(barrier, 20 - 2 * at_home.astype(jnp.int32))

    ORDER = (0, -1, 1)

    def slot(d):
        return blocks.at[d - FAR_LOW]

    def depth_half(ref, half):
        if isinstance(half, int):
            return ref.at[:, :, half * HALF : (half + 1) * HALF]
        return ref.at[:, :, pl.ds(pl.multiple_of(half * HALF, HALF), HALF)]

    def first_copies(distance, part):
        target = -distance
        source = volume.at[:, part * OWN : (part + 1) * OWN]
        into = depth_half(slot(target), gz)
        index = ORDER.index(target)
        remote = pltpu.make_async_remote_copy(
            src_ref=source,
            dst_ref=into,
            send_sem=first_send.at[index, part],
            recv_sem=first_recv.at[index, gz],
            device_id=worker(part, distance),
            device_id_type=MESH,
        )
        return remote, source, into, first_recv.at[index, gz]

    def start_first(distance):
        for part in range(2):
            remote, source, into, recv = first_copies(distance, part)
            if distance == 0:
                here = jnp.logical_and(at_home, core == part)
                pl.when(jnp.logical_not(here))(remote.start)

                @pl.when(here)
                def _(source=source, into=into, recv=recv):
                    pltpu.make_async_copy(source, into, recv).start()

            else:
                remote.start()

    def wait_block(target):
        if target in ORDER:
            for half in range(2):
                into = depth_half(slot(target), half)
                recv = first_recv.at[ORDER.index(target), half]
                pltpu.make_async_copy(into, into, recv).wait()
        else:
            into = slot(target)
            pltpu.make_async_copy(into, into, block_recv.at[target - FAR_LOW]).wait()

    def wait_first_sent(distance):
        index = ORDER.index(-distance)
        for part in range(2):
            source = volume.at[:, part * OWN : (part + 1) * OWN]

            def wait(source=source, part=part):
                pltpu.make_async_copy(source, source, first_send.at[index, part]).wait()

            if distance == 0:
                pl.when(jnp.logical_not(jnp.logical_and(at_home, core == part)))(wait)
            else:
                wait()

    copies = []

    def pass_on(d, distance):
        target = d - distance
        copy = pltpu.make_async_remote_copy(
            src_ref=slot(d),
            dst_ref=slot(target),
            send_sem=block_send.at[target - FAR_LOW],
            recv_sem=block_recv.at[target - FAR_LOW],
            device_id=column_peer(distance),
            device_id_type=MESH,
        )
        copy.start()
        copies.append(copy)

    def take(d, *distances):
        wait_block(d)
        for distance in distances:
            pass_on(d, distance)

    def own_rows(level):
        return pl.ds(LOW[level], OWN)

    def add_block(d, fresh=False):
        source = slot(d)
        for level in range(LEVELS):
            if not REACH[level][0] <= d <= REACH[level][1]:
                continue

            def one(index, carry, level=level):
                total = None
                for cell in range(CELLS):
                    weight = columns[(d - FAR_LOW) * CELLS + cell, level * 8 + index]
                    term = weight * source[cell]
                    total = term if total is None else total + term
                if not fresh:
                    total = total + windows[level][index, own_rows(level)]
                windows[level][index, own_rows(level)] = total
                return carry

            lax.fori_loop(0, 8, one, 0)

    def row_copy(level, number, piece, part):
        block, first, count, into = piece
        run = PARTS[level][part]
        return pltpu.make_async_remote_copy(
            src_ref=windows[level].at[run, pl.ds(LOW[level] + first, count)],
            dst_ref=windows[level].at[run, pl.ds(into, count)],
            send_sem=row_send.at[level, number, part],
            recv_sem=row_recv.at[level, number, part],
            device_id=row_peer(-block),
            device_id_type=MESH,
        )

    rows_sent = []

    def send_rows(level, part=0):
        for number, piece in enumerate(segments(level)):
            copy = row_copy(level, number, piece, part)
            copy.start()
            rows_sent.append((level, part, copy))

    def wait_rows(level, part=0):
        for *owner, copy in rows_sent:
            if owner == [level, part]:
                copy.wait_recv()

    loads[0].wait()
    start_first(1)
    start_first(-1)
    start_first(0)
    loads[1].wait()
    take(-1, 1, -8)
    take(1, -1)
    take(0)
    add_block(0, fresh=True)
    add_block(-1)
    add_block(1)
    send_rows(0)
    take(-2, 1, -8)
    take(2, -1, 8)
    add_block(-2)
    add_block(2)
    take(7)
    add_block(7)
    take(-3, 1, -8)
    take(3, -1, 8)
    add_block(-3)
    add_block(3)
    send_rows(1)
    take(6)
    add_block(6)
    take(-6)
    add_block(-6)
    take(-4)
    add_block(-4)
    take(4)
    add_block(4)
    take(5)
    add_block(5)
    take(-5)
    add_block(-5)
    send_rows(2, 0)
    send_rows(2, 1)

    for load in loads[2:]:
        load.wait()

    def shrink_level(level, part=0):
        span, padded = SPAN[level], PADDED[level]
        low_index, high_index, _ = PARTS[level][part].indices(8)
        lines = pl.ds(low_index * 2 * OWN, (high_index - low_index) * 2 * OWN)

        def rows_forth(index, carry):
            data = windows[level][index]
            if padded > span:
                data = jnp.concatenate(
                    [data, jnp.zeros((padded - span, NZ), jnp.float32)], axis=0
                )
            total = dot(down[level][:, : 3 * padded], stacked(data))
            rows_in[pl.ds(pl.multiple_of(index * 2 * OWN, 2 * OWN), 2 * OWN)] = total
            return carry

        lax.fori_loop(low_index, high_index, rows_forth, 0, unroll=True)
        high, low = split(rows_in[lines])
        bands[lines] = (
            dot(high, depth[level, 0]) + dot(low, depth[level, 0]) + dot(high, depth[level, 1])
        )

        def shrink(index, carry):
            stack = index // 4
            for row_band in range(2):
                first = pl.multiple_of(index * 2 * OWN + row_band * OWN, OWN)
                for depth_band in range(2):
                    number = 4 * stack + 2 * row_band + depth_band
                    limit = limits[level, jnp.maximum(number - 1, 0)]
                    if row_band == 0 and depth_band == 0:
                        none = 0.0 if level == LEVELS - 1 else jnp.inf
                        limit = jnp.where(stack == 0, jnp.float32(none), limit)
                    spot = (pl.ds(first, OWN), pl.ds(depth_band * NZ, NZ))
                    value = bands[spot]
                    value = value - jnp.clip(value, -limit, limit)
                    shrunk_high[spot], shrunk_low[spot] = split(value)
            return carry

        lax.fori_loop(low_index, high_index, shrink, 0, unroll=True)
        rows_out[lines] = (
            dot(shrunk_high[lines], back[level, 0])
            + dot(shrunk_low[lines], back[level, 0])
            + dot(shrunk_high[lines], back[level, 1])
        )

        def rows_back(index, carry):
            data = rows_out[pl.ds(pl.multiple_of(index * 2 * OWN, 2 * OWN), 2 * OWN)]
            total = dot(up[level][:padded, : 6 * OWN], stacked(data))
            spreads[level][index] = total[:span]
            return carry

        lax.fori_loop(low_index, high_index, rows_back, 0, unroll=True)

    back_sent = []

    def send_back(level, part=0):
        run = PARTS[level][part]
        for number, (block, _, count, into) in enumerate(segments(level)):
            copy = pltpu.make_async_remote_copy(
                src_ref=spreads[level].at[run, pl.ds(into, count)],
                dst_ref=landed.at[level, number, run, pl.ds(0, count)],
                send_sem=back_send.at[level, number, part],
                recv_sem=back_recv.at[level, number, part],
                device_id=row_peer(block),
                device_id_type=MESH,
            )
            copy.start()
            back_sent.append((level, copy))

    def gather_back(level):
        for owner, copy in back_sent:
            if owner == level:
                copy.wait_recv()

        def one(index, carry):
            for group in range(OWN // 8):
                total = spreads[level][index, pl.ds(LOW[level] + group * 8, 8)]
                for number, (_, first, count, _) in enumerate(segments(level)):
                    if first <= group * 8 < first + count:
                        total = total + landed[level, number, index, pl.ds(group * 8 - first, 8)]
                stacks[level, index, pl.ds(group * 8, 8)] = total
            return carry

        lax.fori_loop(0, 8, one, 0)

    wait_rows(0)
    shrink_level(0)
    wait_rows(1)
    shrink_level(1)
    wait_rows(2, 0)
    shrink_level(2, 0)
    send_back(2, 0)
    wait_rows(2, 1)
    shrink_level(2, 1)
    send_back(2, 1)
    send_back(1)
    send_back(0)
    gather_back(2)

    def term(d):
        return terms.at[d - FAR_LOW]

    def fill(d):
        target = term(d)

        def one(cell, carry):
            total = None
            for level in range(LEVELS):
                if not REACH[level][0] <= d <= REACH[level][1]:
                    continue
                for index in range(8):
                    weight = columns[(d - FAR_LOW) * CELLS + cell, level * 8 + index]
                    product = weight * stacks[level, index]
                    total = product if total is None else total + product
            target[cell] = total
            return carry

        lax.fori_loop(0, CELLS, one, 0)

    UP3, UP2, UP1, DN3, DN2, DN1, HI5, HI6, HI7, LO5, LO6 = range(11)
    SAME, UP0, DN0 = range(3)
    moved = []

    def hand_on(source, target, distance):
        copy = pltpu.make_async_remote_copy(
            src_ref=source,
            dst_ref=sums.at[target],
            send_sem=sum_send.at[target],
            recv_sem=sum_recv.at[target],
            device_id=column_peer(distance),
            device_id_type=MESH,
        )
        copy.start()
        moved.append(copy)
        return copy

    def arrived(which):
        spot = sums.at[which]
        pltpu.make_async_copy(spot, spot, sum_recv.at[which]).wait()
        return spot

    def join(d, which):
        term(d)[...] = term(d)[...] + arrived(which)[...]

    def add_term(which, d):
        spot = arrived(which)
        spot[...] = spot[...] + term(d)[...]
        return spot

    def deliver(source, which, distance):
        into = finals.at[which, :, pl.ds(pl.multiple_of(core * OWN, OWN), OWN)]
        for half in range(2):
            part = depth_half(source, half)
            remote = pltpu.make_async_remote_copy(
                src_ref=part,
                dst_ref=into,
                send_sem=final_send.at[which, half],
                recv_sem=final_recv.at[which, core],
                device_id=holder(half, distance),
                device_id_type=MESH,
            )
            if which == SAME:
                here = jnp.logical_and(at_home, gz == half)
                pl.when(jnp.logical_not(here))(remote.start)

                @pl.when(here)
                def _(part=part):
                    pltpu.make_async_copy(part, into, final_recv.at[which, core]).start()

            else:
                remote.start()

    def wait_delivered(which):
        for half in range(2):
            part = depth_half(term(0), half)

            def wait(part=part, half=half):
                pltpu.make_async_copy(part, part, final_send.at[which, half]).wait()

            if which == SAME:
                pl.when(jnp.logical_not(jnp.logical_and(at_home, gz == half)))(wait)
            else:
                wait()

    def begin(d, target, distance):
        fill(d)
        hand_on(term(d), target, distance)

    begin(5, HI5, 8)
    begin(-5, LO5, -8)
    begin(4, UP3, 1)
    begin(-4, DN3, -1)
    gather_back(1)
    fill(3)
    fill(-3)
    fill(6)
    fill(-6)
    join(3, LO5)
    hand_on(add_term(UP3, 3), UP2, 1)
    join(-3, HI5)
    hand_on(add_term(DN3, -3), DN2, -1)
    hand_on(term(6), HI6, 8)
    hand_on(term(-6), LO6, -8)
    fill(2)
    fill(-2)
    fill(7)
    join(2, LO6)
    hand_on(add_term(UP2, 2), UP1, 1)
    join(-2, HI6)
    hand_on(add_term(DN2, -2), DN1, -1)
    hand_on(term(7), HI7, 8)
    gather_back(0)
    fill(0)
    deliver(term(0), SAME, 0)
    fill(1)
    fill(-1)
    deliver(add_term(UP1, 1), UP0, 1)
    join(-1, HI7)
    deliver(add_term(DN1, -1), DN0, -1)
    total = None
    for which in (SAME, UP0, DN0):
        for part in range(2):
            spot = finals.at[which, :, pl.ds(part * OWN, OWN)]
            pltpu.make_async_copy(spot, spot, final_recv.at[which, part]).wait()
        total = finals[which] if total is None else total + finals[which]
    result[...] = total

    for distance in (-1, 0, 1):
        wait_first_sent(distance)
    for copy in copies:
        copy.wait_send()
    for *_, copy in rows_sent + back_sent:
        copy.wait_send()
    for copy in moved:
        copy.wait_send()
    for which in range(3):
        wait_delivered(which)


def per_device(volume, thresholds):
    columns, down, up, depth, back = tables()
    block = (CELLS, OWN, NZ)
    f32, bf16 = jnp.float32, jnp.bfloat16
    vmem, dma = pltpu.VMEM, pltpu.SemaphoreType.DMA
    window_shapes = [vmem((8, span, NZ), f32) for span in SPAN]
    count = FAR_HIGH - FAR_LOW + 1
    return pl.pallas_call(
        kernel,
        out_shape=pltpu.VMEM(volume.shape, volume.dtype),
        in_specs=[pl.BlockSpec(memory_space=pltpu.HBM)] * 7,
        out_specs=pl.BlockSpec(memory_space=pltpu.VMEM),
        scratch_shapes=[
            vmem(volume.shape, f32),
            pltpu.SMEM(thresholds.shape, f32),
            pltpu.SMEM(columns.shape[1:], f32),
            vmem(down.shape[1:], bf16),
            vmem(up.shape[1:], bf16),
            vmem(depth.shape, bf16),
            vmem(back.shape, bf16),
            vmem((count,) + block, f32),
            *window_shapes,
            *window_shapes,
            vmem((LEVELS, 4, 8, OWN, NZ), f32),
            vmem((LEVELS, 8, OWN, NZ), f32),
            vmem((16 * OWN, NZ), f32),
            vmem((16 * OWN, 2 * NZ), f32),
            vmem((16 * OWN, 2 * NZ), bf16),
            vmem((16 * OWN, 2 * NZ), bf16),
            vmem((16 * OWN, NZ), f32),
            vmem((count,) + block, f32),
            vmem((11,) + block, f32),
            vmem((3,) + volume.shape, f32),
            dma((7,)),
            dma((3, 2)),
            dma((3, 2)),
            dma((count,)),
            dma((count,)),
            dma((LEVELS, 4, 2)),
            dma((LEVELS, 4, 2)),
            dma((LEVELS, 4, 2)),
            dma((LEVELS, 4, 2)),
            dma((11,)),
            dma((11,)),
            dma((3, 2)),
            dma((3, 2)),
        ],
        compiler_params=pltpu.CompilerParams(
            collective_id=0, has_side_effects=True, vmem_limit_bytes=60 * 2**20
        ),
        name="shrinkage",
    )(thresholds, volume, columns, down, up, depth, back)


def solution(mesh):
    placed = (P("gx", "gy", "gz"), P())
    return jax.shard_map(
        per_device, mesh=mesh, in_specs=placed, out_specs=P("gx", "gy", "gz"), check_vma=False
    )
```

```python
import math

import jax
import jax.numpy as jnp
import ml_dtypes
import numpy as np
from jax import lax
from jax.experimental import pallas as pl
from jax.experimental.pallas import tpu as pltpu
from jax.sharding import PartitionSpec as P

MESH = pl.DeviceIdType.MESH
LEVELS = 3
NX, NY, NZ = 128, 256, 256
GX, GY, GZ = 32, 8, 2
CELLS = NX // GX
ROWS = NY // GY
HALF = NZ // GZ
OWN = ROWS // GZ

base_taps = [
    0.23037781330885523,
    0.7148465705525415,
    0.6308807679295904,
    -0.02798376941698385,
    -0.18703481171888114,
    0.030841381835986965,
    0.032883011666982945,
    -0.010597401784997278,
]
scaling_taps = [value / math.sqrt(2.0) for value in base_taps]
wavelet_taps = [(-1.0) ** index * base_taps[7 - index] / math.sqrt(2.0) for index in range(8)]

FAR_LOW, FAR_HIGH = -6, 7
REACH = ((-1, 1), (-3, 3), (FAR_LOW, FAR_HIGH))
LOW = (8, 16, 24)
SPAN = (32, 48, 72)
PADDED = (32, 48, 80)
PARTS = ((slice(0, 8),), (slice(0, 8),), (slice(0, 4), slice(4, 8)))


def chains(count):
    def banded(taps, step):
        out = np.zeros((count, count))
        for index, tap in enumerate(taps):
            offset = (index - 3) * step
            rows = np.arange(max(0, -offset), min(count, count - offset))
            out[rows, rows + offset] = tap
        return out

    so_far, result = np.eye(count), []
    for level in range(LEVELS):
        low = banded(scaling_taps, 2**level) @ so_far
        high = banded(wavelet_taps, 2**level) @ so_far
        result.append((low, high))
        so_far = low
    return result


def two_parts(table):
    high = table.astype(ml_dtypes.bfloat16)
    low = (table - high.astype(np.float64)).astype(ml_dtypes.bfloat16)
    return high, low


def tables():
    columns = np.zeros((GX, (FAR_HIGH - FAR_LOW + 1) * CELLS, 128), np.float32)
    for level, pair in enumerate(chains(NX)):
        for band, matrix in enumerate(pair):
            for device in range(GX):
                for cell in range(CELLS):
                    for place in range(columns.shape[1]):
                        source = (device + FAR_LOW) * CELLS + place
                        if 0 <= source < NX:
                            columns[device, place, level * 8 + band * 4 + cell] = matrix[
                                device * CELLS + cell, source
                            ]
    down = np.zeros((GY * GZ, LEVELS, 2 * OWN, 256), ml_dtypes.bfloat16)
    up = np.zeros((GY * GZ, LEVELS, PADDED[2], 128), ml_dtypes.bfloat16)
    for level, pair in enumerate(chains(NY)):
        for device in range(GY * GZ):
            window = np.zeros((2, OWN, PADDED[level]))
            for place in range(SPAN[level]):
                source = device * OWN - LOW[level] + place
                if 0 <= source < NY:
                    for band in range(2):
                        window[band, :, place] = pair[band][
                            device * OWN : device * OWN + OWN, source
                        ]
            window = window.reshape(2 * OWN, PADDED[level])
            high, low = two_parts(window)
            down[device, level, :, : 3 * PADDED[level]] = np.concatenate([high, high, low], axis=1)
            up[device, level, : PADDED[level], : 6 * OWN] = np.concatenate([high, high, low]).T
    depth = np.zeros((LEVELS, 2, NZ, 2 * NZ), ml_dtypes.bfloat16)
    depth_back = np.zeros((LEVELS, 2, 2 * NZ, NZ), ml_dtypes.bfloat16)
    for level, pair in enumerate(chains(NZ)):
        both = np.concatenate(pair, axis=0)
        for part, value in enumerate(two_parts(both)):
            depth_back[level, part] = value
            depth[level, part] = value.T
    return columns, down, up, depth, depth_back


def segments(level):
    start, stop = -LOW[level], SPAN[level] - LOW[level]
    pieces = []
    for block in (-2, -1, 1, 2):
        low, high = max(start, block * OWN), min(stop, (block + 1) * OWN)
        if low < high:
            pieces.append((block, low - block * OWN, high - low, low - start))
    return pieces


def split(value):
    high = value.astype(jnp.bfloat16)
    return high, (value - high.astype(jnp.float32)).astype(jnp.bfloat16)


def stacked(value):
    high, low = split(value)
    return jnp.concatenate([high, low, high], axis=0)


def dot(a, b):
    return jnp.dot(a, b, preferred_element_type=jnp.float32)


def kernel(
    limits_hbm,
    volume_hbm,
    columns_hbm,
    down_hbm,
    up_hbm,
    depth_hbm,
    back_hbm,
    result,
    volume,
    limits,
    columns,
    down,
    up,
    depth,
    back,
    blocks,
    window0,
    window1,
    window2,
    spread0,
    spread1,
    spread2,
    landed,
    stacks,
    rows_in,
    bands,
    shrunk_high,
    shrunk_low,
    rows_out,
    terms,
    sums,
    finals,
    load_sem,
    first_send,
    first_recv,
    block_send,
    block_recv,
    row_send,
    row_recv,
    back_send,
    back_recv,
    sum_send,
    sum_recv,
    final_send,
    final_recv,
):
    gz, gy, gx = lax.axis_index("gz"), lax.axis_index("gy"), lax.axis_index("gx")
    pair, core = gy // 2, lax.rem(gy, 2)
    windows = (window0, window1, window2)
    spreads = (spread0, spread1, spread2)

    place = 4 * pair + 2 * gz + core
    at_home = gz == core

    def column_of(distance):
        return lax.rem(gx + distance + GX, GX)

    def column_peer(distance):
        return (gz, gy, column_of(distance))

    def worker(part, distance):
        return (core, 2 * pair + part, column_of(distance))

    def holder(half, distance):
        return (half, 2 * pair + gz, column_of(distance))

    def row_peer(block):
        other = lax.rem(place + block + 16, 16)
        return (lax.rem(other // 2, 2), 2 * (other // 4) + lax.rem(other, 2), gx)

    loads = [
        pltpu.make_async_copy(source, target, load_sem.at[index])
        for index, (source, target) in enumerate(
            (
                (volume_hbm, volume),
                (columns_hbm.at[gx], columns),
                (limits_hbm, limits),
                (down_hbm.at[place], down),
                (up_hbm.at[place], up),
                (depth_hbm, depth),
                (back_hbm, back),
            )
        )
    ]
    loads[0].start()

    barrier = pltpu.get_barrier_semaphore()

    def greet(peer):
        pl.semaphore_signal(barrier, inc=1, device_id=peer, device_id_type=MESH)

    for part in range(2):
        for distance in (-1, 1):
            greet(worker(part, distance))
            greet(holder(part, distance))
        pl.when(jnp.logical_not(jnp.logical_and(at_home, core == part)))(
            lambda part=part: greet(worker(part, 0))
        )
        pl.when(jnp.logical_not(jnp.logical_and(at_home, gz == part)))(
            lambda part=part: greet(holder(part, 0))
        )
    for distance in (-8, -1, 1, 8):
        greet(column_peer(distance))
    for block in (-2, -1, 1, 2):
        greet(row_peer(block))
    for load in loads[1:]:
        load.start()
    pl.semaphore_wait(barrier, 20 - 2 * at_home.astype(jnp.int32))

    ORDER = (0, -1, 1)

    def slot(d):
        return blocks.at[d - FAR_LOW]

    def depth_half(ref, half):
        if isinstance(half, int):
            return ref.at[:, :, half * HALF : (half + 1) * HALF]
        return ref.at[:, :, pl.ds(pl.multiple_of(half * HALF, HALF), HALF)]

    def first_copies(distance, part):
        target = -distance
        source = volume.at[:, part * OWN : (part + 1) * OWN]
        into = depth_half(slot(target), gz)
        index = ORDER.index(target)
        remote = pltpu.make_async_remote_copy(
            src_ref=source,
            dst_ref=into,
            send_sem=first_send.at[index, part],
            recv_sem=first_recv.at[index, gz],
            device_id=worker(part, distance),
            device_id_type=MESH,
        )
        return remote, source, into, first_recv.at[index, gz]

    def start_first(distance):
        for part in range(2):
            remote, source, into, recv = first_copies(distance, part)
            if distance == 0:
                here = jnp.logical_and(at_home, core == part)
                pl.when(jnp.logical_not(here))(remote.start)

                @pl.when(here)
                def _(source=source, into=into, recv=recv):
                    pltpu.make_async_copy(source, into, recv).start()

            else:
                remote.start()

    def wait_block(target):
        if target in ORDER:
            for half in range(2):
                into = depth_half(slot(target), half)
                recv = first_recv.at[ORDER.index(target), half]
                pltpu.make_async_copy(into, into, recv).wait()
        else:
            into = slot(target)
            pltpu.make_async_copy(into, into, block_recv.at[target - FAR_LOW]).wait()

    def wait_first_sent(distance):
        index = ORDER.index(-distance)
        for part in range(2):
            source = volume.at[:, part * OWN : (part + 1) * OWN]

            def wait(source=source, part=part):
                pltpu.make_async_copy(source, source, first_send.at[index, part]).wait()

            if distance == 0:
                pl.when(jnp.logical_not(jnp.logical_and(at_home, core == part)))(wait)
            else:
                wait()

    copies = []

    def pass_on(d, distance):
        target = d - distance
        copy = pltpu.make_async_remote_copy(
            src_ref=slot(d),
            dst_ref=slot(target),
            send_sem=block_send.at[target - FAR_LOW],
            recv_sem=block_recv.at[target - FAR_LOW],
            device_id=column_peer(distance),
            device_id_type=MESH,
        )
        copy.start()
        copies.append(copy)

    def take(d, *distances):
        wait_block(d)
        for distance in distances:
            pass_on(d, distance)

    def own_rows(level):
        return pl.ds(LOW[level], OWN)

    def add_block(d, fresh=False):
        source = slot(d)
        for level in range(LEVELS):
            if not REACH[level][0] <= d <= REACH[level][1]:
                continue

            def one(index, carry, level=level):
                total = None
                for cell in range(CELLS):
                    weight = columns[(d - FAR_LOW) * CELLS + cell, level * 8 + index]
                    term = weight * source[cell]
                    total = term if total is None else total + term
                if not fresh:
                    total = total + windows[level][index, own_rows(level)]
                windows[level][index, own_rows(level)] = total
                return carry

            lax.fori_loop(0, 8, one, 0, unroll=4)

    def row_copy(level, number, piece, part):
        block, first, count, into = piece
        run = PARTS[level][part]
        return pltpu.make_async_remote_copy(
            src_ref=windows[level].at[run, pl.ds(LOW[level] + first, count)],
            dst_ref=windows[level].at[run, pl.ds(into, count)],
            send_sem=row_send.at[level, number, part],
            recv_sem=row_recv.at[level, number, part],
            device_id=row_peer(-block),
            device_id_type=MESH,
        )

    rows_sent = []

    def send_rows(level, part=0):
        for number, piece in enumerate(segments(level)):
            copy = row_copy(level, number, piece, part)
            copy.start()
            rows_sent.append((level, part, copy))

    def wait_rows(level, part=0):
        for *owner, copy in rows_sent:
            if owner == [level, part]:
                copy.wait_recv()

    loads[0].wait()
    start_first(1)
    start_first(-1)
    start_first(0)
    loads[1].wait()
    take(-1, 1, -8)
    take(1, -1)
    take(0)
    add_block(0, fresh=True)
    add_block(-1)
    add_block(1)
    send_rows(0)
    take(-2, 1, -8)
    take(2, -1, 8)
    add_block(-2)
    add_block(2)
    take(7)
    add_block(7)
    take(-3, 1, -8)
    take(3, -1, 8)
    add_block(-3)
    add_block(3)
    send_rows(1)
    take(6)
    add_block(6)
    take(-6)
    add_block(-6)
    take(-4)
    add_block(-4)
    take(4)
    add_block(4)
    take(5)
    add_block(5)
    take(-5)
    add_block(-5)
    send_rows(2, 0)
    send_rows(2, 1)

    for load in loads[2:]:
        load.wait()

    def shrink_level(level, part=0):
        span, padded = SPAN[level], PADDED[level]
        low_index, high_index, _ = PARTS[level][part].indices(8)
        lines = pl.ds(low_index * 2 * OWN, (high_index - low_index) * 2 * OWN)

        def rows_forth(index, carry):
            data = windows[level][index]
            if padded > span:
                data = jnp.concatenate(
                    [data, jnp.zeros((padded - span, NZ), jnp.float32)], axis=0
                )
            total = dot(down[level][:, : 3 * padded], stacked(data))
            rows_in[pl.ds(pl.multiple_of(index * 2 * OWN, 2 * OWN), 2 * OWN)] = total
            return carry

        lax.fori_loop(low_index, high_index, rows_forth, 0, unroll=True)
        high, low = split(rows_in[lines])
        bands[lines] = (
            dot(high, depth[level, 0]) + dot(low, depth[level, 0]) + dot(high, depth[level, 1])
        )

        def shrink(index, carry):
            stack = index // 4
            for row_band in range(2):
                first = pl.multiple_of(index * 2 * OWN + row_band * OWN, OWN)
                for depth_band in range(2):
                    number = 4 * stack + 2 * row_band + depth_band
                    limit = limits[level, jnp.maximum(number - 1, 0)]
                    if row_band == 0 and depth_band == 0:
                        none = 0.0 if level == LEVELS - 1 else jnp.inf
                        limit = jnp.where(stack == 0, jnp.float32(none), limit)
                    spot = (pl.ds(first, OWN), pl.ds(depth_band * NZ, NZ))
                    value = bands[spot]
                    value = value - jnp.clip(value, -limit, limit)
                    shrunk_high[spot], shrunk_low[spot] = split(value)
            return carry

        lax.fori_loop(low_index, high_index, shrink, 0, unroll=True)
        rows_out[lines] = (
            dot(shrunk_high[lines], back[level, 0])
            + dot(shrunk_low[lines], back[level, 0])
            + dot(shrunk_high[lines], back[level, 1])
        )

        def rows_back(index, carry):
            data = rows_out[pl.ds(pl.multiple_of(index * 2 * OWN, 2 * OWN), 2 * OWN)]
            total = dot(up[level][:padded, : 6 * OWN], stacked(data))
            spreads[level][index] = total[:span]
            return carry

        lax.fori_loop(low_index, high_index, rows_back, 0, unroll=True)

    back_sent = []

    def send_back(level, part=0):
        run = PARTS[level][part]
        for number, (block, _, count, into) in enumerate(segments(level)):
            copy = pltpu.make_async_remote_copy(
                src_ref=spreads[level].at[run, pl.ds(into, count)],
                dst_ref=landed.at[level, number, run, pl.ds(0, count)],
                send_sem=back_send.at[level, number, part],
                recv_sem=back_recv.at[level, number, part],
                device_id=row_peer(block),
                device_id_type=MESH,
            )
            copy.start()
            back_sent.append((level, copy))

    def gather_back(level):
        for owner, copy in back_sent:
            if owner == level:
                copy.wait_recv()

        def one(index, carry):
            for group in range(OWN // 8):
                total = spreads[level][index, pl.ds(LOW[level] + group * 8, 8)]
                for number, (_, first, count, _) in enumerate(segments(level)):
                    if first <= group * 8 < first + count:
                        total = total + landed[level, number, index, pl.ds(group * 8 - first, 8)]
                stacks[level, index, pl.ds(group * 8, 8)] = total
            return carry

        lax.fori_loop(0, 8, one, 0)

    wait_rows(0)
    shrink_level(0)
    wait_rows(1)
    shrink_level(1)
    wait_rows(2, 0)
    shrink_level(2, 0)
    send_back(2, 0)
    wait_rows(2, 1)
    shrink_level(2, 1)
    send_back(2, 1)
    send_back(1)
    send_back(0)
    gather_back(2)

    def term(d):
        return terms.at[d - FAR_LOW]

    def fill(d):
        target = term(d)

        def one(cell, carry):
            total = None
            for level in range(LEVELS):
                if not REACH[level][0] <= d <= REACH[level][1]:
                    continue
                for index in range(8):
                    weight = columns[(d - FAR_LOW) * CELLS + cell, level * 8 + index]
                    product = weight * stacks[level, index]
                    total = product if total is None else total + product
            target[cell] = total
            return carry

        lax.fori_loop(0, CELLS, one, 0, unroll=2)

    UP3, UP2, UP1, DN3, DN2, DN1, HI5, HI6, HI7, LO5, LO6 = range(11)
    SAME, UP0, DN0 = range(3)
    moved = []

    def hand_on(source, target, distance):
        copy = pltpu.make_async_remote_copy(
            src_ref=source,
            dst_ref=sums.at[target],
            send_sem=sum_send.at[target],
            recv_sem=sum_recv.at[target],
            device_id=column_peer(distance),
            device_id_type=MESH,
        )
        copy.start()
        moved.append(copy)
        return copy

    def arrived(which):
        spot = sums.at[which]
        pltpu.make_async_copy(spot, spot, sum_recv.at[which]).wait()
        return spot

    def join(d, which):
        term(d)[...] = term(d)[...] + arrived(which)[...]

    def add_term(which, d):
        spot = arrived(which)
        spot[...] = spot[...] + term(d)[...]
        return spot

    def deliver(source, which, distance):
        into = finals.at[which, :, pl.ds(pl.multiple_of(core * OWN, OWN), OWN)]
        for half in range(2):
            part = depth_half(source, half)
            remote = pltpu.make_async_remote_copy(
                src_ref=part,
                dst_ref=into,
                send_sem=final_send.at[which, half],
                recv_sem=final_recv.at[which, core],
                device_id=holder(half, distance),
                device_id_type=MESH,
            )
            if which == SAME:
                here = jnp.logical_and(at_home, gz == half)
                pl.when(jnp.logical_not(here))(remote.start)

                @pl.when(here)
                def _(part=part):
                    pltpu.make_async_copy(part, into, final_recv.at[which, core]).start()

            else:
                remote.start()

    def wait_delivered(which):
        for half in range(2):
            part = depth_half(term(0), half)

            def wait(part=part, half=half):
                pltpu.make_async_copy(part, part, final_send.at[which, half]).wait()

            if which == SAME:
                pl.when(jnp.logical_not(jnp.logical_and(at_home, gz == half)))(wait)
            else:
                wait()

    def begin(d, target, distance):
        fill(d)
        hand_on(term(d), target, distance)

    begin(5, HI5, 8)
    begin(-5, LO5, -8)
    begin(4, UP3, 1)
    begin(-4, DN3, -1)
    gather_back(1)
    fill(3)
    fill(-3)
    fill(6)
    fill(-6)
    join(3, LO5)
    hand_on(add_term(UP3, 3), UP2, 1)
    join(-3, HI5)
    hand_on(add_term(DN3, -3), DN2, -1)
    hand_on(term(6), HI6, 8)
    hand_on(term(-6), LO6, -8)
    fill(2)
    fill(-2)
    fill(7)
    join(2, LO6)
    hand_on(add_term(UP2, 2), UP1, 1)
    join(-2, HI6)
    hand_on(add_term(DN2, -2), DN1, -1)
    hand_on(term(7), HI7, 8)
    gather_back(0)
    fill(0)
    deliver(term(0), SAME, 0)
    fill(1)
    fill(-1)
    deliver(add_term(UP1, 1), UP0, 1)
    join(-1, HI7)
    deliver(add_term(DN1, -1), DN0, -1)
    total = None
    for which in (SAME, UP0, DN0):
        for part in range(2):
            spot = finals.at[which, :, pl.ds(part * OWN, OWN)]
            pltpu.make_async_copy(spot, spot, final_recv.at[which, part]).wait()
        total = finals[which] if total is None else total + finals[which]
    result[...] = total

    for distance in (-1, 0, 1):
        wait_first_sent(distance)
    for copy in copies:
        copy.wait_send()
    for *_, copy in rows_sent + back_sent:
        copy.wait_send()
    for copy in moved:
        copy.wait_send()
    for which in range(3):
        wait_delivered(which)


def per_device(volume, thresholds):
    columns, down, up, depth, back = tables()
    block = (CELLS, OWN, NZ)
    f32, bf16 = jnp.float32, jnp.bfloat16
    vmem, dma = pltpu.VMEM, pltpu.SemaphoreType.DMA
    window_shapes = [vmem((8, span, NZ), f32) for span in SPAN]
    count = FAR_HIGH - FAR_LOW + 1
    return pl.pallas_call(
        kernel,
        out_shape=pltpu.VMEM(volume.shape, volume.dtype),
        in_specs=[pl.BlockSpec(memory_space=pltpu.HBM)] * 7,
        out_specs=pl.BlockSpec(memory_space=pltpu.VMEM),
        scratch_shapes=[
            vmem(volume.shape, f32),
            pltpu.SMEM(thresholds.shape, f32),
            pltpu.SMEM(columns.shape[1:], f32),
            vmem(down.shape[1:], bf16),
            vmem(up.shape[1:], bf16),
            vmem(depth.shape, bf16),
            vmem(back.shape, bf16),
            vmem((count,) + block, f32),
            *window_shapes,
            *window_shapes,
            vmem((LEVELS, 4, 8, OWN, NZ), f32),
            vmem((LEVELS, 8, OWN, NZ), f32),
            vmem((16 * OWN, NZ), f32),
            vmem((16 * OWN, 2 * NZ), f32),
            vmem((16 * OWN, 2 * NZ), bf16),
            vmem((16 * OWN, 2 * NZ), bf16),
            vmem((16 * OWN, NZ), f32),
            vmem((count,) + block, f32),
            vmem((11,) + block, f32),
            vmem((3,) + volume.shape, f32),
            dma((7,)),
            dma((3, 2)),
            dma((3, 2)),
            dma((count,)),
            dma((count,)),
            dma((LEVELS, 4, 2)),
            dma((LEVELS, 4, 2)),
            dma((LEVELS, 4, 2)),
            dma((LEVELS, 4, 2)),
            dma((11,)),
            dma((11,)),
            dma((3, 2)),
            dma((3, 2)),
        ],
        compiler_params=pltpu.CompilerParams(
            collective_id=0, has_side_effects=True, vmem_limit_bytes=60 * 2**20
        ),
        name="shrinkage",
    )(thresholds, volume, columns, down, up, depth, back)


def solution(mesh):
    placed = (P("gx", "gy", "gz"), P())
    return jax.shard_map(
        per_device, mesh=mesh, in_specs=placed, out_specs=P("gx", "gy", "gz"), check_vma=False
    )
```
